32 devices in a mesh: leaf: 8 (over y, x, core), sib: 4 (over z).
Axes of the slice: x: 2, y: 2, z: 4, core: 2. Of those that a mesh axis runs over, the one named last changes fastest.
Arguments:
- points_x: bfloat16 [32, 524288], P(None, ('leaf', 'sib')), may hold values from -6 to 6
- coords: int32 [2, 524288], P(None, ('leaf', 'sib')), may hold values from 0 to 15, as said below
- near_list: int32 [4096, 9], P(('leaf', 'sib')), may hold values from -1 to 4095, as said below
- leaf_list: int32 [4096, 8], P(('leaf', 'sib')), may hold values from -1 to 4095, as said below
- parent_list: int32 [1024, 27], P(('leaf', 'sib')), may hold values from -1 to 1023, as said below
- basis: bfloat16 [4096, 64, 128], P(('leaf', 'sib')), may hold values from -0.5 to 0.5
- transfer: bfloat16 [1024, 64, 256], P(('leaf', 'sib')), may hold values from -0.375 to 0.375
- leaf_coupling: bfloat16 [4096, 64, 512], P(('leaf', 'sib')), may hold values from -0.25 to 0.25
- parent_coupling: bfloat16 [1024, 64, 1728], P(('leaf', 'sib')), may hold values from -0.15625 to 0.15625
Outputs:
- product: float32 [32, 524288], P(None, ('leaf', 'sib'))
The draws below stay inside these ranges and needn't reach their ends.
Inputs may be any that keep to these rules, and one draw needn't show every extreme that they name: `coords`: both grid indices of every point lie in 0 to 15. `near_list`: slot k of leaf t is t + (k // 3 - 1) * 128 + k % 3 - 1 or -1; it is -1 where that patch lies outside the grid of rows of 128 leaves; the middle slot is always t. `leaf_list`: each entry is -1 or a leaf of the same aligned group of 512 leaves as t; slot 0 is never -1. `parent_list`: each parent's list holds 1 to 27 valid entries first and -1 after them; some parent has all 27.
All inputs are finite; a program needn't handle non-finite values.
Results may differ from the reference program's by a relative error of at most 0.0023.
Values may be sent and summed in bfloat16 or wider, within the bound.
No kernel may reach another device: no remote copies, remote signals or barrier semaphores. Data moves between devices by JAX's collectives and lax.ppermute only.
A program may use at most 192 MiB of HBM per device.

```python
import math
import jax
import jax.numpy as jnp
from jax import lax

R = 32
LEAF = 128
RANK = 64
NEAR = 9
CL = 8
CP = 27
LEAVES_DEV = 128
PAR_DEV = 32
GROUP_LEAVES = 512
NL = 4096
NP = 1024
NPTS = 524288


def draw_coords(key, part):
    first_key, second_key = jax.random.split(jax.random.fold_in(key, 11))
    number = jnp.arange(NPTS, dtype=jnp.int32)
    across = jax.random.randint(first_key, (NPTS,), 0, 16, dtype=jnp.int32)
    across = jnp.where(number == NPTS - 1, 15, across)
    upward = jax.random.randint(second_key, (NPTS,), 0, 16, dtype=jnp.int32)
    return jnp.stack([across, upward]).astype(jnp.int32)


def draw_near_list(key, part):
    leaf_ids = jnp.arange(NL, dtype=jnp.int32)[:, None]
    slot_ids = jnp.arange(NEAR, dtype=jnp.int32)[None, :]
    step_y = slot_ids // 3 - 1
    step_x = slot_ids % 3 - 1
    column = leaf_ids % LEAVES_DEV + step_x
    row = leaf_ids // LEAVES_DEV + step_y
    sources = leaf_ids + step_y * LEAVES_DEV + step_x
    keep = jax.random.randint(jax.random.fold_in(key, 21), (NL, NEAR), 0, 4, dtype=jnp.int32) > 0
    keep = jnp.logical_or(keep, slot_ids == NEAR // 2)
    inside = jnp.logical_and(jnp.logical_and(column >= 0, column < LEAVES_DEV), jnp.logical_and(row >= 0, row < NL // LEAVES_DEV))
    return jnp.where(jnp.logical_and(keep, inside), sources, -1).astype(jnp.int32)


def draw_leaf_list(key, part):
    pick_key, keep_key = jax.random.split(jax.random.fold_in(key, 31))
    leaf_ids = jnp.arange(NL, dtype=jnp.int32)[:, None]
    slot_ids = jnp.arange(CL, dtype=jnp.int32)[None, :]
    group_base = leaf_ids // GROUP_LEAVES * GROUP_LEAVES
    sources = group_base + jax.random.randint(pick_key, (NL, CL), 0, GROUP_LEAVES, dtype=jnp.int32)
    keep = jax.random.randint(keep_key, (NL, CL), 0, 4, dtype=jnp.int32) > 0
    keep = jnp.logical_or(keep, slot_ids == 0)
    chosen = jnp.where(keep, sources, -1)
    chosen = jnp.where(jnp.logical_and(leaf_ids == NL - 1, slot_ids == 0), NL - 1, chosen)
    chosen = jnp.where(jnp.logical_and(leaf_ids == 0, slot_ids == CL - 1), -1, chosen)
    return chosen.astype(jnp.int32)


def draw_parent_list(key, part):
    heavy_key, light_key, pick_key = jax.random.split(jax.random.fold_in(key, 41), 3)
    device_count = NP // PAR_DEV
    parent_ids = jnp.arange(NP, dtype=jnp.int32)
    heavy = jax.random.randint(heavy_key, (device_count,), 0, 4, dtype=jnp.int32) == 0
    heavy_here = heavy[parent_ids // PAR_DEV]
    light = jax.random.randint(light_key, (NP,), 1, CP // 2 + 1, dtype=jnp.int32)
    filled = jnp.where(jnp.logical_or(heavy_here, parent_ids == 0), CP, light)
    sources = jax.random.randint(pick_key, (NP, CP), 0, NP, dtype=jnp.int32)
    slot_ids = jnp.arange(CP, dtype=jnp.int32)[None, :]
    sources = jnp.where(jnp.logical_and(parent_ids[:, None] == NP - 1, slot_ids == 0), NP - 1, sources)
    return jnp.where(slot_ids < filled[:, None], sources, -1).astype(jnp.int32)


def levels(stream_key, extent, shards, least, high):
    def one(axis_at, shards_of):
        draws = jax.random.uniform(jax.random.fold_in(jax.random.fold_in(stream_key, 6), axis_at), (shards_of,), jnp.float32, least / len(shards), high / len(shards))
        return jnp.repeat(jnp.exp(draws), extent[axis_at] // shards_of).reshape((-1,) + (1,) * (len(extent) - axis_at - 1))

    gain = one(*shards[0])
    for cut in shards[1:]:
        gain = gain * one(*cut)
    return gain


def normal_values(own_key, extent, width, reach, cuts=(), kind=jnp.bfloat16):
    factor_of = levels(own_key, extent, cuts, -0.22, 0.18) if cuts else 1.0
    result = jax.random.normal(own_key, extent, jnp.float32) * width * factor_of
    return jnp.minimum(jnp.maximum(result, -reach), reach).astype(kind)


def setup_inputs(seed: int = 0) -> dict:
    seeds = jax.random.split(jax.random.key(seed), 10)
    points_x = normal_values(seeds[0], (R, NPTS), 1.0, 6.0, ((1, 32),))
    coords = draw_coords(jax.random.fold_in(seeds[9], 71), 0)
    near_list = draw_near_list(jax.random.fold_in(seeds[9], 71), 0)
    leaf_list = draw_leaf_list(jax.random.fold_in(seeds[9], 71), 0)
    parent_list = draw_parent_list(jax.random.fold_in(seeds[9], 71), 0)
    basis = normal_values(seeds[5], (NL, RANK, LEAF), LEAF ** -0.5, 0.5, ((0, 32),))
    transfer = normal_values(seeds[6], (NP, RANK, 4 * RANK), (4 * RANK) ** -0.5, 0.375, ((0, 32),))
    leaf_coupling = normal_values(seeds[7], (NL, RANK, CL * RANK), (CL * RANK) ** -0.5, 0.25, ((0, 32),))
    parent_coupling = normal_values(seeds[8], (NP, RANK, CP * RANK), (CP * RANK) ** -0.5, 0.15625, ((0, 32),))
    return dict(points_x=points_x, coords=coords, near_list=near_list, leaf_list=leaf_list, parent_list=parent_list, basis=basis, transfer=transfer, leaf_coupling=leaf_coupling, parent_coupling=parent_coupling)


def couple_block(lookup, indices, blocks):
    count, slots = indices.shape
    present = indices >= 0
    sources = jnp.take(lookup, jnp.clip(indices, 0, lookup.shape[0] - 1).astype(jnp.int32), axis=0)
    sources = jnp.where(present[:, :, None, None], sources.astype(jnp.float32), jnp.float32(0.0))
    sources = sources.transpose(0, 2, 1, 3).reshape(count, R, slots * RANK)
    return jnp.einsum('trj,taj->tra', sources, blocks.astype(jnp.float32))

def reference(points_x, coords, near_list, leaf_list, parent_list, basis, transfer, leaf_coupling, parent_coupling):
    point_rows = points_x.reshape(R, NL, LEAF).transpose(1, 0, 2)
    coord_rows = coords.reshape(2, NL, LEAF).transpose(1, 0, 2)
    leaf_coef = jnp.einsum('trl,tal->tra', point_rows.astype(jnp.float32), basis.astype(jnp.float32)).astype(jnp.bfloat16)
    children = leaf_coef.reshape(NP, 4, R, RANK).transpose(0, 2, 1, 3).reshape(NP, R, 4 * RANK)
    parent_coef = jnp.einsum('prj,paj->pra', children.astype(jnp.float32), transfer.astype(jnp.float32)).astype(jnp.bfloat16)
    groups = NL // LEAVES_DEV

    def leaf_step(packed):
        return couple_block(leaf_coef, packed[0], packed[1])
    leaf_far = lax.map(leaf_step, (leaf_list.reshape(groups, LEAVES_DEV, CL), leaf_coupling.reshape(groups, LEAVES_DEV, RANK, CL * RANK)))
    leaf_far = leaf_far.reshape(NL, R, RANK)

    def parent_step(packed):
        return couple_block(parent_coef, packed[0], packed[1])
    parent_far = lax.map(parent_step, (parent_list.reshape(groups, PAR_DEV, CP), parent_coupling.reshape(groups, PAR_DEV, RANK, CP * RANK)))
    parent_far = parent_far.reshape(NP, R, RANK).astype(jnp.bfloat16)
    downward = jnp.einsum('pra,paj->prj', parent_far.astype(jnp.float32), transfer.astype(jnp.float32))
    downward = downward.reshape(NP, R, 4, RANK).transpose(0, 2, 1, 3).reshape(NL, R, RANK)
    leaf_total = (leaf_far + downward).astype(jnp.bfloat16)
    far_field = jnp.einsum('tra,tal->trl', leaf_total.astype(jnp.float32), basis.astype(jnp.float32))
    slot_ids = jnp.arange(NEAR, dtype=jnp.int32)
    shift_x = (-16 * (slot_ids % 3 - 1)).astype(jnp.float32)
    shift_y = (-16 * (slot_ids // 3 - 1)).astype(jnp.float32)

    def near_step(packed):
        indices, target_xy = packed
        present = indices >= 0
        safe = jnp.clip(indices, 0, NL - 1).astype(jnp.int32)
        sources = jnp.take(point_rows, safe, axis=0).astype(jnp.float32)
        source_xy = jnp.take(coord_rows, safe, axis=0)
        delta_x = (target_xy[:, None, 0, :, None] - source_xy[:, :, 0, None, :]).astype(jnp.float32) + shift_x[None, :, None, None]
        delta_y = (target_xy[:, None, 1, :, None] - source_xy[:, :, 1, None, :]).astype(jnp.float32) + shift_y[None, :, None, None]
        kernel_block = 4.0 / (math.pi * jnp.sqrt(delta_x * delta_x + delta_y * delta_y + 0.25))
        kernel_block = jnp.where(present[:, :, None, None], kernel_block, jnp.float32(0.0)).astype(jnp.bfloat16)
        return jnp.einsum('tkij,tkrj->tri', kernel_block.astype(jnp.float32), sources)
    near_field = lax.map(near_step, (near_list.reshape(groups, LEAVES_DEV, NEAR), coord_rows.reshape(groups, LEAVES_DEV, 2, LEAF)))
    near_field = near_field.reshape(NL, R, LEAF)
    return (far_field + near_field).transpose(1, 0, 2).reshape(R, NPTS)
```

```python
import functools
import math

import jax
import jax.numpy as jnp
import numpy as np
from jax import lax
from jax.experimental import pallas as pl
from jax.experimental.pallas import tpu as pltpu
from jax.sharding import PartitionSpec as P

CELLS = 256
NT = (((1,), (1,)), ((), ()))
NN = (((1,), (0,)), ((), ()))
VMEM_LIMIT = 56 * 1024 * 1024


def dot(a, b, dims):
    return lax.dot_general(a, b, dims, preferred_element_type=jnp.float32)


def kernel_table():
    cell = np.arange(CELLS)
    at_x, at_y = cell % 16, cell // 16
    blocks = []
    for step_y in range(-1, 2):
        for step_x in range(-1, 2):
            dx = (at_x[None, :] - at_x[:, None] - 16 * step_x).astype(np.float32)
            dy = (at_y[None, :] - at_y[:, None] - 16 * step_y).astype(np.float32)
            root = np.sqrt(dx * dx + dy * dy + np.float32(0.25))
            blocks.append(np.float32(4.0) / (np.float32(math.pi) * root))
    return np.stack(blocks).reshape(3, 3 * CELLS, CELLS).astype(jnp.bfloat16)


def low_lanes(rows):
    return lax.broadcasted_iota(jnp.int32, (rows, 128), 1) < 64


def one_hot(cells):
    hit = lax.broadcasted_iota(jnp.int32, (CELLS, cells.shape[1]), 0) == cells
    return jnp.where(hit, jnp.float32(1), jnp.float32(0)).astype(jnp.bfloat16)


def split(v):
    high = v.astype(jnp.bfloat16)
    low = (v - high.astype(jnp.float32)).astype(jnp.bfloat16)
    return high, low


def diagonal(y, sides):
    low = low_lanes(sides)
    left = jnp.where(low, y[:sides, :128], y[sides : 2 * sides, :128])
    right = jnp.where(low, y[2 * sides : 3 * sides, 128:], y[3 * sides :, 128:])
    return jnp.concatenate([left, right], axis=1)


def coef_kernel(x_ref, basis_ref, transfer_ref, leaf_ref, parent_ref):
    sides = x_ref.shape[0]
    low = low_lanes(sides)
    for pair in range(leaf_ref.shape[0] // 2):
        rows = []
        for p in (2 * pair, 2 * pair + 1):
            x4 = jnp.concatenate(
                [x_ref[:, (4 * p + c) * 128 : (4 * p + c + 1) * 128] for c in range(4)], axis=0
            )
            y = dot(x4, basis_ref[4 * p : 4 * p + 4].reshape(256, 128), NT)
            coef = diagonal(y, sides).astype(jnp.bfloat16)
            leaf_ref[p] = coef
            rows.append(coef)
        z = dot(
            jnp.concatenate(rows, axis=0),
            transfer_ref[2 * pair : 2 * pair + 2].reshape(128, 256),
            NT,
        )
        parent_ref[pair] = jnp.where(low, z[:sides], z[sides:]).astype(jnp.bfloat16)


def coefficients(x, basis, transfer):
    sides, parents = x.shape[0], transfer.shape[0]
    step = 8
    return pl.pallas_call(
        coef_kernel,
        grid=(parents // step,),
        in_specs=[
            pl.BlockSpec((sides, step * 512), lambda g: (0, g)),
            pl.BlockSpec((step * 4, 64, 128), lambda g: (g, 0, 0)),
            pl.BlockSpec((step, 64, 256), lambda g: (g, 0, 0)),
        ],
        out_specs=[
            pl.BlockSpec((step, sides, 256), lambda g: (g, 0, 0)),
            pl.BlockSpec((step // 2, sides, 128), lambda g: (g, 0, 0)),
        ],
        out_shape=[
            jax.ShapeDtypeStruct((parents, sides, 256), jnp.bfloat16),
            jax.ShapeDtypeStruct((parents // 2, sides, 128), jnp.bfloat16),
        ],
        compiler_params=pltpu.CompilerParams(vmem_limit_bytes=VMEM_LIMIT),
        cost_estimate=pl.CostEstimate(
            flops=600_000_000, bytes_accessed=5_000_000, transcendentals=0
        ),
        name="coefficients",
    )(x, basis, transfer)


def near_kernel(index_ref, x_ref, cells_ref, table_ref, *rest):
    *u_in, u_ref, charge_ref, lhs_ref = rest
    sides = x_ref.shape[0]
    leaves = cells_ref.shape[0]
    step = u_ref.shape[0]
    g = pl.program_id(0)

    @pl.when(g == 0)
    def _():
        charge_ref[leaves] = jnp.zeros(charge_ref.shape[1:], jnp.bfloat16)

        def group(first, carry):
            for extra in range(8):
                t = first * 8 + extra
                hot = one_hot(cells_ref[pl.ds(t, 1), :])
                y = dot(x_ref[:, pl.ds(pl.multiple_of(t * 128, 128), 128)], hot, NT)
                high, low = split(y)
                charge_ref[t, :sides] = high
                charge_ref[t, sides:] = low
            return carry

        lax.fori_loop(0, leaves // 8, group, 0)

    for t in range(step):
        for k in range(3):
            lhs_ref[t * 2 * sides : (t + 1) * 2 * sides, k * CELLS : (k + 1) * CELLS] = charge_ref[
                index_ref[(g * step + t) * 3 + k]
            ]
    u = dot(lhs_ref[...], table_ref[...], NN).reshape(step, 2 * sides, CELLS)
    u = u[:, :sides] + u[:, sides:]
    if u_in:
        u = u + u_in[0][...]
    u_ref[...] = u


def near_row(index, x, cells, table, u=None):
    sides, leaves = x.shape[0], cells.shape[0]
    step = 16
    block = pl.BlockSpec((step, sides, CELLS), lambda g: (g, 0, 0))
    more = [] if u is None else [u]
    return pl.pallas_call(
        near_kernel,
        grid=(leaves // step,),
        in_specs=[
            pl.BlockSpec(memory_space=pltpu.SMEM),
            pl.BlockSpec((sides, leaves * 128), lambda g: (0, 0)),
            pl.BlockSpec((leaves, 128), lambda g: (0, 0)),
            pl.BlockSpec((3 * CELLS, CELLS), lambda g: (0, 0)),
        ]
        + [block] * len(more),
        out_specs=block,
        out_shape=jax.ShapeDtypeStruct((leaves, sides, CELLS), jnp.float32),
        scratch_shapes=[
            pltpu.VMEM((leaves + 1, 2 * sides, CELLS), jnp.bfloat16),
            pltpu.VMEM((step * 2 * sides, 3 * CELLS), jnp.bfloat16),
        ],
        compiler_params=pltpu.CompilerParams(vmem_limit_bytes=VMEM_LIMIT),
        cost_estimate=pl.CostEstimate(
            flops=9_000_000_000, bytes_accessed=8_000_000, transcendentals=0
        ),
        name="near_row",
    )(index, x, cells, table, *more)


def spread(table_ref, at, pair):
    low = low_lanes(pair.shape[0])
    wide = pair.astype(jnp.float32)
    turned = pltpu.roll(wide, 64, 1)
    table_ref[at] = jnp.where(low, wide, turned).astype(jnp.bfloat16)
    table_ref[at + 1] = jnp.where(low, turned, wide).astype(jnp.bfloat16)


def pick(table_ref, first, second):
    low = low_lanes(table_ref.shape[1])
    return jnp.where(low, table_ref[first], table_ref[second])


def parent_kernel(index_ref, pairs_ref, coupling_ref, transfer_ref, down_ref, table_ref, lhs_ref):
    count, sides, _ = down_ref.shape
    slots = coupling_ref.shape[2] // 64
    pairs = pairs_ref.shape[0]
    low = low_lanes(sides)
    g = pl.program_id(0)

    @pl.when(g == 0)
    def _():
        table_ref[2 * pairs] = jnp.zeros(table_ref.shape[1:], jnp.bfloat16)

        def group(first, carry):
            for extra in range(8):
                at = first * 8 + extra
                spread(table_ref, 2 * at, pairs_ref[at])
            return carry

        lax.fori_loop(0, pairs // 8, group, 0)

    for pair in range(count // 2):
        for half in range(2):
            base = (g * count + 2 * pair + half) * slots
            rows = slice(half * sides, (half + 1) * sides)
            for j in range(slots // 2):
                lhs_ref[rows, j * 128 : (j + 1) * 128] = pick(
                    table_ref, index_ref[base + 2 * j], index_ref[base + 2 * j + 1]
                )
            if slots % 2:
                lhs_ref[rows, slots // 2 * 128 :] = table_ref[index_ref[base + slots - 1]]
        y = dot(
            lhs_ref[:, : slots * 64],
            coupling_ref[2 * pair : 2 * pair + 2].reshape(128, slots * 64),
            NT,
        )
        zero = jnp.zeros((sides, 128), jnp.float32)
        own = jnp.concatenate(
            [jnp.where(low, y[:sides], zero), jnp.where(low, zero, y[sides:])], axis=0
        ).astype(jnp.bfloat16)
        d = dot(own, transfer_ref[2 * pair : 2 * pair + 2].reshape(128, 256), NN)
        down_ref[2 * pair] = d[:sides]
        down_ref[2 * pair + 1] = d[sides:]


def parents_down(index, pairs, coupling, transfer):
    parents, _, width = coupling.shape
    sides = pairs.shape[1]
    step = 8
    return pl.pallas_call(
        parent_kernel,
        grid=(parents // step,),
        in_specs=[
            pl.BlockSpec(memory_space=pltpu.SMEM),
            pl.BlockSpec(pairs.shape, lambda g: (0, 0, 0)),
            pl.BlockSpec((step, 64, width), lambda g: (g, 0, 0)),
            pl.BlockSpec((step, 64, 256), lambda g: (g, 0, 0)),
        ],
        out_specs=pl.BlockSpec((step, sides, 256), lambda g: (g, 0, 0)),
        out_shape=jax.ShapeDtypeStruct((parents, sides, 256), jnp.float32),
        scratch_shapes=[
            pltpu.VMEM((2 * pairs.shape[0] + 1, sides, 128), jnp.bfloat16),
            pltpu.VMEM((2 * sides, (width + 127) // 128 * 128), jnp.bfloat16),
        ],
        compiler_params=pltpu.CompilerParams(vmem_limit_bytes=VMEM_LIMIT),
        cost_estimate=pl.CostEstimate(
            flops=4_000_000_000, bytes_accessed=14_000_000, transcendentals=0
        ),
        name="parents_down",
    )(index, pairs, coupling, transfer)


def final_kernel(pieces, index_ref, *rest):
    piece_refs = rest[:pieces]
    coupling_ref, down_ref, basis_ref, cells_ref, u_ref, out_ref, table_ref, lhs_ref = rest[pieces:]
    parents, sides, _ = down_ref.shape
    slots = coupling_ref.shape[2] // 64
    per_piece = piece_refs[0].shape[0]
    g = pl.program_id(0)

    @pl.when(g == 0)
    def _():
        table_ref[4 * pieces * per_piece] = jnp.zeros(table_ref.shape[1:], jnp.bfloat16)
        for number, piece_ref in enumerate(piece_refs):

            def group(first, carry):
                for extra in range(4):
                    p = first * 4 + extra
                    row = piece_ref[p]
                    at = (number * per_piece + p) * 4
                    spread(table_ref, at, row[:, :128])
                    spread(table_ref, at + 2, row[:, 128:])
                return carry

            lax.fori_loop(0, per_piece // 4, group, 0)

    low = low_lanes(sides)
    for p in range(parents):
        for c in range(4):
            base = (g * parents * 4 + 4 * p + c) * slots
            for j in range(slots // 2):
                lhs_ref[c * sides : (c + 1) * sides, j * 128 : (j + 1) * 128] = pick(
                    table_ref, index_ref[base + 2 * j], index_ref[base + 2 * j + 1]
                )
        y = dot(lhs_ref[...], coupling_ref[4 * p : 4 * p + 4].reshape(256, slots * 64), NT)
        total = diagonal(y, sides) + down_ref[p]
        left, right = total[:, :128], total[:, 128:]
        zero = jnp.zeros((sides, 128), jnp.float32)
        own = jnp.concatenate(
            [
                jnp.concatenate([jnp.where(low, left, zero), zero], axis=1),
                jnp.concatenate([jnp.where(low, zero, left), zero], axis=1),
                jnp.concatenate([zero, jnp.where(low, right, zero)], axis=1),
                jnp.concatenate([zero, jnp.where(low, zero, right)], axis=1),
            ],
            axis=0,
        ).astype(jnp.bfloat16)
        far = dot(own, basis_ref[4 * p : 4 * p + 4].reshape(256, 128), NN)
        for c in range(4):
            t = 4 * p + c
            hot = one_hot(cells_ref[t : t + 1, :])
            near = dot(jnp.concatenate(split(u_ref[t]), axis=0), hot, NN)
            out_ref[:, t * 128 : (t + 1) * 128] = (
                far[c * sides : (c + 1) * sides] + near[:sides] + near[sides:]
            )


def finish(index, pieces, coupling, down, basis, cells, u):
    leaves, _, width = coupling.shape
    sides = down.shape[1]
    step = 16
    whole = pl.BlockSpec(pieces[0].shape, lambda g: (0, 0, 0))
    return pl.pallas_call(
        functools.partial(final_kernel, len(pieces)),
        grid=(leaves // step,),
        in_specs=[pl.BlockSpec(memory_space=pltpu.SMEM)]
        + [whole] * len(pieces)
        + [
            pl.BlockSpec((step, 64, width), lambda g: (g, 0, 0)),
            pl.BlockSpec((step // 4, sides, 256), lambda g: (g, 0, 0)),
            pl.BlockSpec((step, 64, 128), lambda g: (g, 0, 0)),
            pl.BlockSpec((step, 128), lambda g: (g, 0)),
            pl.BlockSpec((step, sides, CELLS), lambda g: (g, 0, 0)),
        ],
        out_specs=pl.BlockSpec((sides, step * 128), lambda g: (0, g)),
        out_shape=jax.ShapeDtypeStruct((sides, leaves * 128), jnp.float32),
        scratch_shapes=[
            pltpu.VMEM((len(pieces) * leaves + 1, sides, 128), jnp.bfloat16),
            pltpu.VMEM((4 * sides, width), jnp.bfloat16),
        ],
        compiler_params=pltpu.CompilerParams(vmem_limit_bytes=VMEM_LIMIT),
        cost_estimate=pl.CostEstimate(
            flops=6_000_000_000, bytes_accessed=20_000_000, transcendentals=0
        ),
        name="finish",
    )(index, *pieces, coupling, down, basis, cells, u)


def body(
    points_x,
    coords,
    near_list,
    leaf_list,
    parent_list,
    basis,
    transfer,
    leaf_coupling,
    parent_coupling,
):
    sides = points_x.shape[0]
    leaves, rank_dim, leaf_size = basis.shape
    parents = leaves // 4
    everyone = ("leaf", "sib")
    devices = lax.axis_size("leaf") * lax.axis_size("sib")
    sibs = lax.axis_size("sib")
    table = jnp.asarray(kernel_table())

    packed_xy = coords.astype(jnp.bfloat16).reshape(sides, -1)
    packed = jnp.concatenate([points_x, packed_xy], axis=1)
    upward = [(i, i + 1) for i in range(devices - 1)]
    downward = [(j, i) for i, j in upward]
    before = lax.ppermute(packed, everyone, upward)
    after = lax.ppermute(packed, everyone, downward)

    leaf_coef, parent_pairs = coefficients(points_x, basis, transfer)
    every_parent = lax.all_gather(parent_pairs, everyone, axis=0, tiled=True)
    pieces = [leaf_coef]
    for shift in range(1, sibs):
        turn = [(i, (i + shift) % sibs) for i in range(sibs)]
        pieces.append(lax.ppermute(leaf_coef, "sib", turn))

    own_cells = (coords[1] * 16 + coords[0]).reshape(leaves, leaf_size)

    def cells_of(other):
        xy = other[:, leaves * leaf_size :].astype(jnp.int32).reshape(2, leaves, leaf_size)
        return xy[1] * 16 + xy[0]

    leaf_ids = jnp.arange(leaves, dtype=jnp.int32)[:, None]
    steps = jnp.arange(3, dtype=jnp.int32)[None, :] - 1
    near_index = jnp.where(
        near_list.reshape(leaves, 3, 3) >= 0, (leaf_ids + steps)[:, None, :], leaves
    )

    def row_index(row):
        return near_index[:, row].reshape(-1)

    me = lax.axis_index("sib")
    group_base = lax.axis_index("leaf") * (sibs * leaves)
    local = leaf_list - group_base
    piece = jnp.bitwise_and(me - local // leaves + sibs, sibs - 1)
    leaf_index = jnp.where(leaf_list >= 0, piece * leaves + local % leaves, sibs * leaves)
    parent_index = jnp.where(parent_list >= 0, parent_list, parents * devices)

    u = near_row(row_index(1), points_x, own_cells, table[1])
    u = near_row(row_index(0), before[:, : leaves * leaf_size], cells_of(before), table[0], u)
    u = near_row(row_index(2), after[:, : leaves * leaf_size], cells_of(after), table[2], u)
    down = parents_down(parent_index.reshape(-1), every_parent, parent_coupling, transfer)
    return finish(
        leaf_index.reshape(-1), pieces, leaf_coupling, down, basis, own_cells, u
    )


def solution(mesh):
    in_specs = (
        P(None, ("leaf", "sib")),
        P(None, ("leaf", "sib")),
        P(("leaf", "sib"), None),
        P(("leaf", "sib"), None),
        P(("leaf", "sib"), None),
        P(("leaf", "sib"), None, None),
        P(("leaf", "sib"), None, None),
        P(("leaf", "sib"), None, None),
        P(("leaf", "sib"), None, None),
    )
    out_specs = P(None, ("leaf", "sib"))
    return jax.shard_map(body, mesh=mesh, in_specs=in_specs, out_specs=out_specs, check_vma=False)
```

```python
import functools
import math

import jax
import jax.numpy as jnp
import numpy as np
from jax import lax
from jax.experimental import pallas as pl
from jax.experimental.pallas import tpu as pltpu
from jax.sharding import PartitionSpec as P

CELLS = 256
NT = (((1,), (1,)), ((), ()))
NN = (((1,), (0,)), ((), ()))
VMEM_LIMIT = 56 * 1024 * 1024


def dot(a, b, dims):
    return lax.dot_general(a, b, dims, preferred_element_type=jnp.float32)


def kernel_table():
    cell = np.arange(CELLS)
    at_x, at_y = cell % 16, cell // 16
    blocks = []
    for step_y in range(-1, 2):
        for step_x in range(-1, 2):
            dx = (at_x[None, :] - at_x[:, None] - 16 * step_x).astype(np.float32)
            dy = (at_y[None, :] - at_y[:, None] - 16 * step_y).astype(np.float32)
            root = np.sqrt(dx * dx + dy * dy + np.float32(0.25))
            blocks.append(np.float32(4.0) / (np.float32(math.pi) * root))
    return np.stack(blocks).reshape(3, 3 * CELLS, CELLS).astype(jnp.bfloat16)


def low_lanes(rows):
    return lax.broadcasted_iota(jnp.int32, (rows, 128), 1) < 64


def one_hot(cells):
    hit = lax.broadcasted_iota(jnp.int32, (CELLS, cells.shape[1]), 0) == cells
    return jnp.where(hit, jnp.float32(1), jnp.float32(0)).astype(jnp.bfloat16)


def split(v):
    high = v.astype(jnp.bfloat16)
    low = (v - high.astype(jnp.float32)).astype(jnp.bfloat16)
    return high, low


def diagonal(y, sides):
    low = low_lanes(sides)
    left = jnp.where(low, y[:sides, :128], y[sides : 2 * sides, :128])
    right = jnp.where(low, y[2 * sides : 3 * sides, 128:], y[3 * sides :, 128:])
    return jnp.concatenate([left, right], axis=1)


def coef_kernel(x_ref, basis_ref, transfer_ref, leaf_ref, parent_ref):
    sides = x_ref.shape[0]
    low = low_lanes(sides)
    for pair in range(leaf_ref.shape[0] // 2):
        rows = []
        for p in (2 * pair, 2 * pair + 1):
            x4 = jnp.concatenate(
                [x_ref[:, (4 * p + c) * 128 : (4 * p + c + 1) * 128] for c in range(4)], axis=0
            )
            y = dot(x4, basis_ref[4 * p : 4 * p + 4].reshape(256, 128), NT)
            coef = diagonal(y, sides).astype(jnp.bfloat16)
            leaf_ref[p] = coef
            rows.append(coef)
        z = dot(
            jnp.concatenate(rows, axis=0),
            transfer_ref[2 * pair : 2 * pair + 2].reshape(128, 256),
            NT,
        )
        parent_ref[pair] = jnp.where(low, z[:sides], z[sides:]).astype(jnp.bfloat16)


def coefficients(x, basis, transfer):
    sides, parents = x.shape[0], transfer.shape[0]
    step = 8
    return pl.pallas_call(
        coef_kernel,
        grid=(parents // step,),
        in_specs=[
            pl.BlockSpec((sides, step * 512), lambda g: (0, g)),
            pl.BlockSpec((step * 4, 64, 128), lambda g: (g, 0, 0)),
            pl.BlockSpec((step, 64, 256), lambda g: (g, 0, 0)),
        ],
        out_specs=[
            pl.BlockSpec((step, sides, 256), lambda g: (g, 0, 0)),
            pl.BlockSpec((step // 2, sides, 128), lambda g: (g, 0, 0)),
        ],
        out_shape=[
            jax.ShapeDtypeStruct((parents, sides, 256), jnp.bfloat16),
            jax.ShapeDtypeStruct((parents // 2, sides, 128), jnp.bfloat16),
        ],
        compiler_params=pltpu.CompilerParams(vmem_limit_bytes=VMEM_LIMIT),
        cost_estimate=pl.CostEstimate(
            flops=1000000, bytes_accessed=1000, transcendentals=0
        ),
        name="coefficients",
    )(x, basis, transfer)


def scatter_row(charge_ref, base, x_ref, cells_ref):
    sides = x_ref.shape[0]

    def group(first, carry):
        for extra in range(8):
            t = first * 8 + extra
            hot = one_hot(cells_ref[pl.ds(t, 1), :])
            y = dot(x_ref[:, pl.ds(pl.multiple_of(t * 128, 128), 128)], hot, NT)
            high, low = split(y)
            charge_ref[base + t, :sides] = high
            charge_ref[base + t, sides:] = low
        return carry

    lax.fori_loop(0, cells_ref.shape[0] // 8, group, 0)


def grid_field(index_ref, charge_ref, lhs_ref, table_ref, first, step):
    sides = charge_ref.shape[1] // 2
    slots = table_ref.shape[0] // CELLS
    for t in range(step):
        for k in range(slots):
            lhs_ref[t * 2 * sides : (t + 1) * 2 * sides, k * CELLS : (k + 1) * CELLS] = charge_ref[
                index_ref[(first + t) * slots + k]
            ]
    u = dot(lhs_ref[...], table_ref[...], NN).reshape(step, 2 * sides, CELLS)
    return u[:, :sides] + u[:, sides:]


def near_own_kernel(index_ref, x_ref, cells_ref, table_ref, u_ref, charge_ref, lhs_ref):
    leaves, step = cells_ref.shape[0], u_ref.shape[0]
    g = pl.program_id(0)

    @pl.when(g == 0)
    def _():
        charge_ref[leaves] = jnp.zeros(charge_ref.shape[1:], jnp.bfloat16)
        scatter_row(charge_ref, 0, x_ref, cells_ref)

    u_ref[...] = grid_field(index_ref, charge_ref, lhs_ref, table_ref, g * step, step)


def near_own(index, x, cells, table):
    sides, leaves = x.shape[0], cells.shape[0]
    step = 16
    return pl.pallas_call(
        near_own_kernel,
        grid=(leaves // step,),
        in_specs=[
            pl.BlockSpec(memory_space=pltpu.SMEM),
            pl.BlockSpec((sides, leaves * 128), lambda g: (0, 0)),
            pl.BlockSpec((leaves, 128), lambda g: (0, 0)),
            pl.BlockSpec(table.shape, lambda g: (0, 0)),
        ],
        out_specs=pl.BlockSpec((step, sides, CELLS), lambda g: (g, 0, 0)),
        out_shape=jax.ShapeDtypeStruct((leaves, sides, CELLS), jnp.float32),
        scratch_shapes=[
            pltpu.VMEM((leaves + 1, 2 * sides, CELLS), jnp.bfloat16),
            pltpu.VMEM((step * 2 * sides, table.shape[0]), jnp.bfloat16),
        ],
        compiler_params=pltpu.CompilerParams(vmem_limit_bytes=VMEM_LIMIT),
        cost_estimate=pl.CostEstimate(
            flops=1000000, bytes_accessed=1000, transcendentals=0
        ),
        name="near_own",
    )(index, x, cells, table)


def near_rest_kernel(
    index_ref, above_ref, below_ref, cells_above_ref, cells_below_ref, table_ref, cells_ref, u_ref, out_ref, charge_ref, lhs_ref
):
    leaves, step = cells_above_ref.shape[0], u_ref.shape[0]
    sides = u_ref.shape[1]
    g = pl.program_id(0)

    @pl.when(g == 0)
    def _():
        charge_ref[2 * leaves] = jnp.zeros(charge_ref.shape[1:], jnp.bfloat16)
        scatter_row(charge_ref, 0, above_ref, cells_above_ref)
        scatter_row(charge_ref, leaves, below_ref, cells_below_ref)

    u = u_ref[...] + grid_field(index_ref, charge_ref, lhs_ref, table_ref, g * step, step)
    for t in range(step):
        hot = one_hot(cells_ref[t : t + 1, :])
        near = dot(jnp.concatenate(split(u[t]), axis=0), hot, NN)
        out_ref[:, t * 128 : (t + 1) * 128] = near[:sides] + near[sides:]


def near_rest(index, above, below, cells_above, cells_below, table, cells, u):
    leaves, sides, _ = u.shape
    step = 16
    row = pl.BlockSpec((sides, leaves * 128), lambda g: (0, 0))
    row_cells = pl.BlockSpec((leaves, 128), lambda g: (0, 0))
    return pl.pallas_call(
        near_rest_kernel,
        grid=(leaves // step,),
        in_specs=[
            pl.BlockSpec(memory_space=pltpu.SMEM),
            row,
            row,
            row_cells,
            row_cells,
            pl.BlockSpec(table.shape, lambda g: (0, 0)),
            pl.BlockSpec((step, 128), lambda g: (g, 0)),
            pl.BlockSpec((step, sides, CELLS), lambda g: (g, 0, 0)),
        ],
        out_specs=pl.BlockSpec((sides, step * 128), lambda g: (0, g)),
        out_shape=jax.ShapeDtypeStruct((sides, leaves * 128), jnp.float32),
        scratch_shapes=[
            pltpu.VMEM((2 * leaves + 1, 2 * sides, CELLS), jnp.bfloat16),
            pltpu.VMEM((step * 2 * sides, table.shape[0]), jnp.bfloat16),
        ],
        compiler_params=pltpu.CompilerParams(vmem_limit_bytes=VMEM_LIMIT),
        cost_estimate=pl.CostEstimate(
            flops=25000000000, bytes_accessed=1000, transcendentals=0
        ),
        name="near_rest",
    )(index, above, below, cells_above, cells_below, table, cells, u)


def spread(table_ref, at, pair):
    low = low_lanes(pair.shape[0])
    wide = pair.astype(jnp.float32)
    turned = pltpu.roll(wide, 64, 1)
    table_ref[at] = jnp.where(low, wide, turned).astype(jnp.bfloat16)
    table_ref[at + 1] = jnp.where(low, turned, wide).astype(jnp.bfloat16)


def pick(table_ref, first, second):
    low = low_lanes(table_ref.shape[1])
    return jnp.where(low, table_ref[first], table_ref[second])


def parent_kernel(pieces, index_ref, *rest):
    pairs_refs = rest[:pieces]
    coupling_ref, transfer_ref, down_ref, table_ref, lhs_ref = rest[pieces:]
    count, sides, _ = down_ref.shape
    slots = coupling_ref.shape[2] // 64
    pairs = pairs_refs[0].shape[0]
    low = low_lanes(sides)
    g = pl.program_id(0)

    @pl.when(g == 0)
    def _():
        table_ref[2 * pieces * pairs] = jnp.zeros(table_ref.shape[1:], jnp.bfloat16)
        for number, pairs_ref in enumerate(pairs_refs):

            def group(first, carry):
                for extra in range(8):
                    at = first * 8 + extra
                    spread(table_ref, 2 * (number * pairs + at), pairs_ref[at])
                return carry

            lax.fori_loop(0, pairs // 8, group, 0)

    for pair in range(count // 2):
        for half in range(2):
            base = (g * count + 2 * pair + half) * slots
            rows = slice(half * sides, (half + 1) * sides)
            for j in range(slots // 2):
                lhs_ref[rows, j * 128 : (j + 1) * 128] = pick(
                    table_ref, index_ref[base + 2 * j], index_ref[base + 2 * j + 1]
                )
            if slots % 2:
                lhs_ref[rows, slots // 2 * 128 :] = table_ref[index_ref[base + slots - 1]]
        y = dot(
            lhs_ref[:, : slots * 64],
            coupling_ref[2 * pair : 2 * pair + 2].reshape(128, slots * 64),
            NT,
        )
        zero = jnp.zeros((sides, 128), jnp.float32)
        own = jnp.concatenate(
            [jnp.where(low, y[:sides], zero), jnp.where(low, zero, y[sides:])], axis=0
        ).astype(jnp.bfloat16)
        d = dot(own, transfer_ref[2 * pair : 2 * pair + 2].reshape(128, 256), NN)
        down_ref[2 * pair] = d[:sides]
        down_ref[2 * pair + 1] = d[sides:]


def parents_down(index, pieces, coupling, transfer):
    parents, _, width = coupling.shape
    pairs, sides, _ = pieces[0].shape
    step = 8
    return pl.pallas_call(
        functools.partial(parent_kernel, len(pieces)),
        grid=(parents // step,),
        in_specs=[
            pl.BlockSpec(memory_space=pltpu.SMEM),
        ]
        + [pl.BlockSpec(pieces[0].shape, lambda g: (0, 0, 0))] * len(pieces)
        + [
            pl.BlockSpec((step, 64, width), lambda g: (g, 0, 0)),
            pl.BlockSpec((step, 64, 256), lambda g: (g, 0, 0)),
        ],
        out_specs=pl.BlockSpec((step, sides, 256), lambda g: (g, 0, 0)),
        out_shape=jax.ShapeDtypeStruct((parents, sides, 256), jnp.float32),
        scratch_shapes=[
            pltpu.VMEM((2 * len(pieces) * pairs + 1, sides, 128), jnp.bfloat16),
            pltpu.VMEM((2 * sides, (width + 127) // 128 * 128), jnp.bfloat16),
        ],
        compiler_params=pltpu.CompilerParams(vmem_limit_bytes=VMEM_LIMIT),
        cost_estimate=pl.CostEstimate(
            flops=17000000000, bytes_accessed=1000, transcendentals=0
        ),
        name="parents_down",
    )(index, *pieces, coupling, transfer)


def final_kernel(pieces, index_ref, *rest):
    piece_refs = rest[:pieces]
    coupling_ref, down_ref, basis_ref, near_ref, out_ref, table_ref, lhs_ref = rest[pieces:]
    parents, sides, _ = down_ref.shape
    slots = coupling_ref.shape[2] // 64
    per_piece = piece_refs[0].shape[0]
    g = pl.program_id(0)

    @pl.when(g == 0)
    def _():
        table_ref[4 * pieces * per_piece] = jnp.zeros(table_ref.shape[1:], jnp.bfloat16)
        for number, piece_ref in enumerate(piece_refs):

            def group(first, carry):
                for extra in range(4):
                    p = first * 4 + extra
                    row = piece_ref[p]
                    at = (number * per_piece + p) * 4
                    spread(table_ref, at, row[:, :128])
                    spread(table_ref, at + 2, row[:, 128:])
                return carry

            lax.fori_loop(0, per_piece // 4, group, 0)

    low = low_lanes(sides)
    for p in range(parents):
        for c in range(4):
            base = (g * parents * 4 + 4 * p + c) * slots
            for j in range(slots // 2):
                lhs_ref[c * sides : (c + 1) * sides, j * 128 : (j + 1) * 128] = pick(
                    table_ref, index_ref[base + 2 * j], index_ref[base + 2 * j + 1]
                )
        y = dot(lhs_ref[...], coupling_ref[4 * p : 4 * p + 4].reshape(256, slots * 64), NT)
        total = diagonal(y, sides) + down_ref[p]
        left, right = total[:, :128], total[:, 128:]
        zero = jnp.zeros((sides, 128), jnp.float32)
        own = jnp.concatenate(
            [
                jnp.concatenate([jnp.where(low, left, zero), zero], axis=1),
                jnp.concatenate([jnp.where(low, zero, left), zero], axis=1),
                jnp.concatenate([zero, jnp.where(low, right, zero)], axis=1),
                jnp.concatenate([zero, jnp.where(low, zero, right)], axis=1),
            ],
            axis=0,
        ).astype(jnp.bfloat16)
        far = dot(own, basis_ref[4 * p : 4 * p + 4].reshape(256, 128), NN)
        for c in range(4):
            columns = slice((4 * p + c) * 128, (4 * p + c + 1) * 128)
            out_ref[:, columns] = far[c * sides : (c + 1) * sides] + near_ref[:, columns]


def finish(index, pieces, coupling, down, basis, near):
    leaves, _, width = coupling.shape
    sides = down.shape[1]
    step = 16
    whole = pl.BlockSpec(pieces[0].shape, lambda g: (0, 0, 0))
    return pl.pallas_call(
        functools.partial(final_kernel, len(pieces)),
        grid=(leaves // step,),
        in_specs=[pl.BlockSpec(memory_space=pltpu.SMEM)]
        + [whole] * len(pieces)
        + [
            pl.BlockSpec((step, 64, width), lambda g: (g, 0, 0)),
            pl.BlockSpec((step // 4, sides, 256), lambda g: (g, 0, 0)),
            pl.BlockSpec((step, 64, 128), lambda g: (g, 0, 0)),
            pl.BlockSpec((sides, step * 128), lambda g: (0, g)),
        ],
        out_specs=pl.BlockSpec((sides, step * 128), lambda g: (0, g)),
        out_shape=jax.ShapeDtypeStruct((sides, leaves * 128), jnp.float32),
        scratch_shapes=[
            pltpu.VMEM((len(pieces) * leaves + 1, sides, 128), jnp.bfloat16),
            pltpu.VMEM((4 * sides, width), jnp.bfloat16),
        ],
        compiler_params=pltpu.CompilerParams(vmem_limit_bytes=VMEM_LIMIT),
        cost_estimate=pl.CostEstimate(
            flops=18000000000, bytes_accessed=1000, transcendentals=0
        ),
        name="finish",
    )(index, *pieces, coupling, down, basis, near)


def gather_parents(pairs):
    sibs, at = lax.axis_size("sib"), lax.axis_index("sib")
    line = [pairs]
    for shift in range(1, sibs):
        turn = [(i, (i + shift) % sibs) for i in range(sibs)]
        line.append(lax.ppermute(pairs, "sib", turn))
    line = jnp.concatenate(line, axis=0)
    every = lax.all_gather(line, "leaf", axis=0, tiled=True)
    return [every], lambda leaf, sib: leaf * sibs + jnp.remainder(at - sib, sibs)


def gather_leaves(block):
    sibs, at = lax.axis_size("sib"), lax.axis_index("sib")
    turns = [
        lax.ppermute(block, "sib", [(i, (i + shift) % sibs) for i in range(sibs)])
        for shift in range(1, sibs)
    ]
    return [block] + turns, lambda sib: jnp.remainder(at - sib, sibs)


def body(
    points_x,
    coords,
    near_list,
    leaf_list,
    parent_list,
    basis,
    transfer,
    leaf_coupling,
    parent_coupling,
):
    sides = points_x.shape[0]
    leaves, rank_dim, leaf_size = basis.shape
    parents = leaves // 4
    everyone = ("leaf", "sib")
    devices = lax.axis_size("leaf") * lax.axis_size("sib")
    sibs = lax.axis_size("sib")
    table = jnp.asarray(kernel_table())

    packed_xy = coords.astype(jnp.bfloat16).reshape(sides, -1)
    packed = jnp.concatenate([points_x, packed_xy], axis=1)
    upward = [(i, i + 1) for i in range(devices - 1)]
    downward = [(j, i) for i, j in upward]
    before = lax.ppermute(packed, everyone, upward)
    after = lax.ppermute(packed, everyone, downward)

    leaf_coef, parent_pairs = coefficients(points_x, basis, transfer)
    parent_pieces, parent_place = gather_parents(parent_pairs)

    own_cells = (coords[1] * 16 + coords[0]).reshape(leaves, leaf_size)

    def cells_of(other):
        xy = other[:, leaves * leaf_size :].astype(jnp.int32).reshape(2, leaves, leaf_size)
        return xy[1] * 16 + xy[0]

    leaf_ids = jnp.arange(leaves, dtype=jnp.int32)[:, None]
    steps = jnp.arange(3, dtype=jnp.int32)[None, :] - 1
    own_list = near_list[:, 3:6]
    own_index = jnp.where(own_list >= 0, leaf_ids + steps, leaves)
    rest_list = jnp.concatenate([near_list[:, :3], near_list[:, 6:]], axis=1)
    rest_place = jnp.concatenate([leaf_ids + steps, leaves + leaf_ids + steps], axis=1)
    rest_index = jnp.where(rest_list >= 0, rest_place, 2 * leaves)

    owner = parent_list // parents
    parent_index = jnp.where(
        parent_list >= 0,
        parent_place(owner // sibs, owner % sibs) * parents + parent_list % parents,
        devices * parents,
    )

    def indices_of_leaves(leaf_place, leaf_pieces):
        local = leaf_list - lax.axis_index("leaf") * (sibs * leaves)
        return jnp.where(
            leaf_list >= 0,
            leaf_place(local // leaves) * leaves + local % leaves,
            len(leaf_pieces) * leaves,
        )

    u = near_own(own_index.reshape(-1), points_x, own_cells, table[1])
    leaf_coef, _ = lax.optimization_barrier((leaf_coef, (before, after)))
    leaf_pieces, leaf_place = gather_leaves(leaf_coef)
    leaf_index = indices_of_leaves(leaf_place, leaf_pieces)
    near = near_rest(
        rest_index.reshape(-1),
        before,
        after,
        cells_of(before),
        cells_of(after),
        jnp.concatenate([table[0], table[2]], axis=0),
        own_cells,
        u,
    )
    down = parents_down(parent_index.reshape(-1), parent_pieces, parent_coupling, transfer)
    return finish(leaf_index.reshape(-1), leaf_pieces, leaf_coupling, down, basis, near)


def solution(mesh):
    in_specs = (
        P(None, ("leaf", "sib")),
        P(None, ("leaf", "sib")),
        P(("leaf", "sib"), None),
        P(("leaf", "sib"), None),
        P(("leaf", "sib"), None),
        P(("leaf", "sib"), None, None),
        P(("leaf", "sib"), None, None),
        P(("leaf", "sib"), None, None),
        P(("leaf", "sib"), None, None),
    )
    out_specs = P(None, ("leaf", "sib"))
    return jax.shard_map(body, mesh=mesh, in_specs=in_specs, out_specs=out_specs, check_vma=False)
```

```python
import functools
import math

import jax
import jax.numpy as jnp
import numpy as np
from jax import lax
from jax.experimental import pallas as pl
from jax.experimental.pallas import tpu as pltpu
from jax.sharding import PartitionSpec as P

CELLS = 256
NT = (((1,), (1,)), ((), ()))
NN = (((1,), (0,)), ((), ()))
VMEM_LIMIT = 56 * 1024 * 1024


def dot(a, b, dims):
    return lax.dot_general(a, b, dims, preferred_element_type=jnp.float32)


def kernel_table():
    cell = np.arange(CELLS)
    at_x, at_y = cell % 16, cell // 16
    blocks = []
    for step_y in range(-1, 2):
        for step_x in range(-1, 2):
            dx = (at_x[None, :] - at_x[:, None] - 16 * step_x).astype(np.float32)
            dy = (at_y[None, :] - at_y[:, None] - 16 * step_y).astype(np.float32)
            root = np.sqrt(dx * dx + dy * dy + np.float32(0.25))
            blocks.append(np.float32(4.0) / (np.float32(math.pi) * root))
    return np.stack(blocks).reshape(3, 3 * CELLS, CELLS).astype(jnp.bfloat16)


def low_lanes(rows):
    return lax.broadcasted_iota(jnp.int32, (rows, 128), 1) < 64


def one_hot(cells):
    hit = lax.broadcasted_iota(jnp.int32, (CELLS, cells.shape[1]), 0) == cells
    return jnp.where(hit, jnp.float32(1), jnp.float32(0)).astype(jnp.bfloat16)


def split(v):
    high = v.astype(jnp.bfloat16)
    low = (v - high.astype(jnp.float32)).astype(jnp.bfloat16)
    return high, low


def diagonal(y, sides):
    low = low_lanes(sides)
    left = jnp.where(low, y[:sides, :128], y[sides : 2 * sides, :128])
    right = jnp.where(low, y[2 * sides : 3 * sides, 128:], y[3 * sides :, 128:])
    return jnp.concatenate([left, right], axis=1)


def coef_kernel(x_ref, basis_ref, transfer_ref, leaf_ref, parent_ref):
    sides = x_ref.shape[0]
    low = low_lanes(sides)
    for pair in range(leaf_ref.shape[0] // 2):
        rows = []
        for p in (2 * pair, 2 * pair + 1):
            x4 = jnp.concatenate(
                [x_ref[:, (4 * p + c) * 128 : (4 * p + c + 1) * 128] for c in range(4)], axis=0
            )
            y = dot(x4, basis_ref[4 * p : 4 * p + 4].reshape(256, 128), NT)
            coef = diagonal(y, sides).astype(jnp.bfloat16)
            leaf_ref[p] = coef
            rows.append(coef)
        z = dot(
            jnp.concatenate(rows, axis=0),
            transfer_ref[2 * pair : 2 * pair + 2].reshape(128, 256),
            NT,
        )
        parent_ref[pair] = jnp.where(low, z[:sides], z[sides:]).astype(jnp.bfloat16)


def coefficients(x, basis, transfer):
    sides, parents = x.shape[0], transfer.shape[0]
    step = 8
    return pl.pallas_call(
        coef_kernel,
        grid=(parents // step,),
        in_specs=[
            pl.BlockSpec((sides, step * 512), lambda g: (0, g)),
            pl.BlockSpec((step * 4, 64, 128), lambda g: (g, 0, 0)),
            pl.BlockSpec((step, 64, 256), lambda g: (g, 0, 0)),
        ],
        out_specs=[
            pl.BlockSpec((step, sides, 256), lambda g: (g, 0, 0)),
            pl.BlockSpec((step // 2, sides, 128), lambda g: (g, 0, 0)),
        ],
        out_shape=[
            jax.ShapeDtypeStruct((parents, sides, 256), jnp.bfloat16),
            jax.ShapeDtypeStruct((parents // 2, sides, 128), jnp.bfloat16),
        ],
        compiler_params=pltpu.CompilerParams(vmem_limit_bytes=VMEM_LIMIT),
        cost_estimate=pl.CostEstimate(
            flops=1000000, bytes_accessed=1000, transcendentals=0
        ),
        name="coefficients",
    )(x, basis, transfer)


def scatter_row(charge_ref, base, x_ref, cells_ref):
    sides = x_ref.shape[0]

    def group(first, carry):
        for extra in range(8):
            t = first * 8 + extra
            hot = one_hot(cells_ref[pl.ds(t, 1), :])
            y = dot(x_ref[:, pl.ds(pl.multiple_of(t * 128, 128), 128)], hot, NT)
            high, low = split(y)
            charge_ref[base + t, :sides] = high
            charge_ref[base + t, sides:] = low
        return carry

    lax.fori_loop(0, cells_ref.shape[0] // 8, group, 0)


def grid_field(index_ref, charge_ref, lhs_ref, table_ref, first, step):
    sides = charge_ref.shape[1] // 2
    slots = table_ref.shape[0] // CELLS
    for t in range(step):
        for k in range(slots):
            lhs_ref[t * 2 * sides : (t + 1) * 2 * sides, k * CELLS : (k + 1) * CELLS] = charge_ref[
                index_ref[(first + t) * slots + k]
            ]
    u = dot(lhs_ref[...], table_ref[...], NN).reshape(step, 2 * sides, CELLS)
    return u[:, :sides] + u[:, sides:]


def near_own_kernel(index_ref, x_ref, cells_ref, table_ref, u_ref, charge_ref, lhs_ref):
    leaves, step = cells_ref.shape[0], u_ref.shape[0]
    g = pl.program_id(0)

    @pl.when(g == 0)
    def _():
        charge_ref[leaves] = jnp.zeros(charge_ref.shape[1:], jnp.bfloat16)
        scatter_row(charge_ref, 0, x_ref, cells_ref)

    u_ref[...] = grid_field(index_ref, charge_ref, lhs_ref, table_ref, g * step, step)


def near_own(index, x, cells, table):
    sides, leaves = x.shape[0], cells.shape[0]
    step = 32
    return pl.pallas_call(
        near_own_kernel,
        grid=(leaves // step,),
        in_specs=[
            pl.BlockSpec(memory_space=pltpu.SMEM),
            pl.BlockSpec((sides, leaves * 128), lambda g: (0, 0)),
            pl.BlockSpec((leaves, 128), lambda g: (0, 0)),
            pl.BlockSpec(table.shape, lambda g: (0, 0)),
        ],
        out_specs=pl.BlockSpec((step, sides, CELLS), lambda g: (g, 0, 0)),
        out_shape=jax.ShapeDtypeStruct((leaves, sides, CELLS), jnp.float32),
        scratch_shapes=[
            pltpu.VMEM((leaves + 1, 2 * sides, CELLS), jnp.bfloat16),
            pltpu.VMEM((step * 2 * sides, table.shape[0]), jnp.bfloat16),
        ],
        compiler_params=pltpu.CompilerParams(vmem_limit_bytes=VMEM_LIMIT),
        cost_estimate=pl.CostEstimate(
            flops=1000000, bytes_accessed=1000, transcendentals=0
        ),
        name="near_own",
    )(index, x, cells, table)


def near_rest_kernel(
    index_ref, above_ref, below_ref, cells_above_ref, cells_below_ref, table_ref, cells_ref, u_ref, out_ref, charge_ref, lhs_ref
):
    leaves, step = cells_above_ref.shape[0], u_ref.shape[0]
    sides = u_ref.shape[1]
    g = pl.program_id(0)

    @pl.when(g == 0)
    def _():
        charge_ref[2 * leaves] = jnp.zeros(charge_ref.shape[1:], jnp.bfloat16)
        scatter_row(charge_ref, 0, above_ref, cells_above_ref)
        scatter_row(charge_ref, leaves, below_ref, cells_below_ref)

    u = u_ref[...] + grid_field(index_ref, charge_ref, lhs_ref, table_ref, g * step, step)
    for t in range(step):
        hot = one_hot(cells_ref[t : t + 1, :])
        near = dot(jnp.concatenate(split(u[t]), axis=0), hot, NN)
        out_ref[:, t * 128 : (t + 1) * 128] = near[:sides] + near[sides:]


def near_rest(index, above, below, cells_above, cells_below, table, cells, u):
    leaves, sides, _ = u.shape
    step = 32
    row = pl.BlockSpec((sides, leaves * 128), lambda g: (0, 0))
    row_cells = pl.BlockSpec((leaves, 128), lambda g: (0, 0))
    return pl.pallas_call(
        near_rest_kernel,
        grid=(leaves // step,),
        in_specs=[
            pl.BlockSpec(memory_space=pltpu.SMEM),
            row,
            row,
            row_cells,
            row_cells,
            pl.BlockSpec(table.shape, lambda g: (0, 0)),
            pl.BlockSpec((step, 128), lambda g: (g, 0)),
            pl.BlockSpec((step, sides, CELLS), lambda g: (g, 0, 0)),
        ],
        out_specs=pl.BlockSpec((sides, step * 128), lambda g: (0, g)),
        out_shape=jax.ShapeDtypeStruct((sides, leaves * 128), jnp.float32),
        scratch_shapes=[
            pltpu.VMEM((2 * leaves + 1, 2 * sides, CELLS), jnp.bfloat16),
            pltpu.VMEM((step * 2 * sides, table.shape[0]), jnp.bfloat16),
        ],
        compiler_params=pltpu.CompilerParams(vmem_limit_bytes=VMEM_LIMIT),
        cost_estimate=pl.CostEstimate(
            flops=25000000000, bytes_accessed=1000, transcendentals=0
        ),
        name="near_rest",
    )(index, above, below, cells_above, cells_below, table, cells, u)


def spread(table_ref, at, pair):
    low = low_lanes(pair.shape[0])
    wide = pair.astype(jnp.float32)
    turned = pltpu.roll(wide, 64, 1)
    table_ref[at] = jnp.where(low, wide, turned).astype(jnp.bfloat16)
    table_ref[at + 1] = jnp.where(low, turned, wide).astype(jnp.bfloat16)


def pick(table_ref, first, second):
    low = low_lanes(table_ref.shape[1])
    return jnp.where(low, table_ref[first], table_ref[second])


def parent_kernel(pieces, index_ref, *rest):
    pairs_refs = rest[:pieces]
    coupling_ref, transfer_ref, down_ref, table_ref, lhs_ref = rest[pieces:]
    count, sides, _ = down_ref.shape
    slots = coupling_ref.shape[2] // 64
    pairs = pairs_refs[0].shape[0]
    low = low_lanes(sides)
    g = pl.program_id(0)

    @pl.when(g == 0)
    def _():
        table_ref[2 * pieces * pairs] = jnp.zeros(table_ref.shape[1:], jnp.bfloat16)
        for number, pairs_ref in enumerate(pairs_refs):

            def group(first, carry):
                for extra in range(8):
                    at = first * 8 + extra
                    spread(table_ref, 2 * (number * pairs + at), pairs_ref[at])
                return carry

            lax.fori_loop(0, pairs // 8, group, 0)

    for pair in range(count // 2):
        for half in range(2):
            base = (g * count + 2 * pair + half) * slots
            rows = slice(half * sides, (half + 1) * sides)
            for j in range(slots // 2):
                lhs_ref[rows, j * 128 : (j + 1) * 128] = pick(
                    table_ref, index_ref[base + 2 * j], index_ref[base + 2 * j + 1]
                )
            if slots % 2:
                lhs_ref[rows, slots // 2 * 128 :] = table_ref[index_ref[base + slots - 1]]
        y = dot(
            lhs_ref[:, : slots * 64],
            coupling_ref[2 * pair : 2 * pair + 2].reshape(128, slots * 64),
            NT,
        )
        zero = jnp.zeros((sides, 128), jnp.float32)
        own = jnp.concatenate(
            [jnp.where(low, y[:sides], zero), jnp.where(low, zero, y[sides:])], axis=0
        ).astype(jnp.bfloat16)
        d = dot(own, transfer_ref[2 * pair : 2 * pair + 2].reshape(128, 256), NN)
        down_ref[2 * pair] = d[:sides]
        down_ref[2 * pair + 1] = d[sides:]


def parents_down(index, pieces, coupling, transfer):
    parents, _, width = coupling.shape
    pairs, sides, _ = pieces[0].shape
    step = 8
    return pl.pallas_call(
        functools.partial(parent_kernel, len(pieces)),
        grid=(parents // step,),
        in_specs=[
            pl.BlockSpec(memory_space=pltpu.SMEM),
        ]
        + [pl.BlockSpec(pieces[0].shape, lambda g: (0, 0, 0))] * len(pieces)
        + [
            pl.BlockSpec((step, 64, width), lambda g: (g, 0, 0)),
            pl.BlockSpec((step, 64, 256), lambda g: (g, 0, 0)),
        ],
        out_specs=pl.BlockSpec((step, sides, 256), lambda g: (g, 0, 0)),
        out_shape=jax.ShapeDtypeStruct((parents, sides, 256), jnp.float32),
        scratch_shapes=[
            pltpu.VMEM((2 * len(pieces) * pairs + 1, sides, 128), jnp.bfloat16),
            pltpu.VMEM((2 * sides, (width + 127) // 128 * 128), jnp.bfloat16),
        ],
        compiler_params=pltpu.CompilerParams(vmem_limit_bytes=VMEM_LIMIT),
        cost_estimate=pl.CostEstimate(
            flops=17000000000, bytes_accessed=1000, transcendentals=0
        ),
        name="parents_down",
    )(index, *pieces, coupling, transfer)


def final_kernel(pieces, index_ref, *rest):
    piece_refs = rest[:pieces]
    coupling_ref, down_ref, basis_ref, near_ref, out_ref, table_ref, lhs_ref = rest[pieces:]
    parents, sides, _ = down_ref.shape
    slots = coupling_ref.shape[2] // 64
    per_piece = piece_refs[0].shape[0]
    g = pl.program_id(0)

    @pl.when(g == 0)
    def _():
        table_ref[4 * pieces * per_piece] = jnp.zeros(table_ref.shape[1:], jnp.bfloat16)
        for number, piece_ref in enumerate(piece_refs):

            def group(first, carry):
                for extra in range(4):
                    p = first * 4 + extra
                    row = piece_ref[p]
                    at = (number * per_piece + p) * 4
                    spread(table_ref, at, row[:, :128])
                    spread(table_ref, at + 2, row[:, 128:])
                return carry

            lax.fori_loop(0, per_piece // 4, group, 0)

    low = low_lanes(sides)
    for p in range(parents):
        for c in range(4):
            base = (g * parents * 4 + 4 * p + c) * slots
            for j in range(slots // 2):
                lhs_ref[c * sides : (c + 1) * sides, j * 128 : (j + 1) * 128] = pick(
                    table_ref, index_ref[base + 2 * j], index_ref[base + 2 * j + 1]
                )
        y = dot(lhs_ref[...], coupling_ref[4 * p : 4 * p + 4].reshape(256, slots * 64), NT)
        total = diagonal(y, sides) + down_ref[p]
        left, right = total[:, :128], total[:, 128:]
        zero = jnp.zeros((sides, 128), jnp.float32)
        own = jnp.concatenate(
            [
                jnp.concatenate([jnp.where(low, left, zero), zero], axis=1),
                jnp.concatenate([jnp.where(low, zero, left), zero], axis=1),
                jnp.concatenate([zero, jnp.where(low, right, zero)], axis=1),
                jnp.concatenate([zero, jnp.where(low, zero, right)], axis=1),
            ],
            axis=0,
        ).astype(jnp.bfloat16)
        far = dot(own, basis_ref[4 * p : 4 * p + 4].reshape(256, 128), NN)
        for c in range(4):
            columns = slice((4 * p + c) * 128, (4 * p + c + 1) * 128)
            out_ref[:, columns] = far[c * sides : (c + 1) * sides] + near_ref[:, columns]


def finish(index, pieces, coupling, down, basis, near):
    leaves, _, width = coupling.shape
    sides = down.shape[1]
    step = 32
    whole = pl.BlockSpec(pieces[0].shape, lambda g: (0, 0, 0))
    return pl.pallas_call(
        functools.partial(final_kernel, len(pieces)),
        grid=(leaves // step,),
        in_specs=[pl.BlockSpec(memory_space=pltpu.SMEM)]
        + [whole] * len(pieces)
        + [
            pl.BlockSpec((step, 64, width), lambda g: (g, 0, 0)),
            pl.BlockSpec((step // 4, sides, 256), lambda g: (g, 0, 0)),
            pl.BlockSpec((step, 64, 128), lambda g: (g, 0, 0)),
            pl.BlockSpec((sides, step * 128), lambda g: (0, g)),
        ],
        out_specs=pl.BlockSpec((sides, step * 128), lambda g: (0, g)),
        out_shape=jax.ShapeDtypeStruct((sides, leaves * 128), jnp.float32),
        scratch_shapes=[
            pltpu.VMEM((len(pieces) * leaves + 1, sides, 128), jnp.bfloat16),
            pltpu.VMEM((4 * sides, width), jnp.bfloat16),
        ],
        compiler_params=pltpu.CompilerParams(vmem_limit_bytes=VMEM_LIMIT),
        cost_estimate=pl.CostEstimate(
            flops=18000000000, bytes_accessed=1000, transcendentals=0
        ),
        name="finish",
    )(index, *pieces, coupling, down, basis, near)


def gather_parents(pairs):
    sibs, at = lax.axis_size("sib"), lax.axis_index("sib")
    line = [pairs]
    for shift in range(1, sibs):
        turn = [(i, (i + shift) % sibs) for i in range(sibs)]
        line.append(lax.ppermute(pairs, "sib", turn))
    line = jnp.concatenate(line, axis=0)
    every = lax.all_gather(line, "leaf", axis=0, tiled=True)
    return [every], lambda leaf, sib: leaf * sibs + jnp.remainder(at - sib, sibs)


def gather_leaves(block):
    sibs, at = lax.axis_size("sib"), lax.axis_index("sib")
    turns = [
        lax.ppermute(block, "sib", [(i, (i + shift) % sibs) for i in range(sibs)])
        for shift in range(1, sibs)
    ]
    return [block] + turns, lambda sib: jnp.remainder(at - sib, sibs)


def body(
    points_x,
    coords,
    near_list,
    leaf_list,
    parent_list,
    basis,
    transfer,
    leaf_coupling,
    parent_coupling,
):
    sides = points_x.shape[0]
    leaves, rank_dim, leaf_size = basis.shape
    parents = leaves // 4
    everyone = ("leaf", "sib")
    devices = lax.axis_size("leaf") * lax.axis_size("sib")
    sibs = lax.axis_size("sib")
    table = jnp.asarray(kernel_table())

    packed_xy = coords.astype(jnp.bfloat16).reshape(sides, -1)
    packed = jnp.concatenate([points_x, packed_xy], axis=1)
    upward = [(i, i + 1) for i in range(devices - 1)]
    downward = [(j, i) for i, j in upward]
    before = lax.ppermute(packed, everyone, upward)
    after = lax.ppermute(packed, everyone, downward)

    leaf_coef, parent_pairs = coefficients(points_x, basis, transfer)
    parent_pieces, parent_place = gather_parents(parent_pairs)

    own_cells = (coords[1] * 16 + coords[0]).reshape(leaves, leaf_size)

    def cells_of(other):
        xy = other[:, leaves * leaf_size :].astype(jnp.int32).reshape(2, leaves, leaf_size)
        return xy[1] * 16 + xy[0]

    leaf_ids = jnp.arange(leaves, dtype=jnp.int32)[:, None]
    steps = jnp.arange(3, dtype=jnp.int32)[None, :] - 1
    own_list = near_list[:, 3:6]
    own_index = jnp.where(own_list >= 0, leaf_ids + steps, leaves)
    rest_list = jnp.concatenate([near_list[:, :3], near_list[:, 6:]], axis=1)
    rest_place = jnp.concatenate([leaf_ids + steps, leaves + leaf_ids + steps], axis=1)
    rest_index = jnp.where(rest_list >= 0, rest_place, 2 * leaves)

    owner = parent_list // parents
    parent_index = jnp.where(
        parent_list >= 0,
        parent_place(owner // sibs, owner % sibs) * parents + parent_list % parents,
        devices * parents,
    )

    def indices_of_leaves(leaf_place, leaf_pieces):
        local = leaf_list - lax.axis_index("leaf") * (sibs * leaves)
        return jnp.where(
            leaf_list >= 0,
            leaf_place(local // leaves) * leaves + local % leaves,
            len(leaf_pieces) * leaves,
        )

    u = near_own(own_index.reshape(-1), points_x, own_cells, table[1])
    leaf_coef, _ = lax.optimization_barrier((leaf_coef, (before, after)))
    leaf_pieces, leaf_place = gather_leaves(leaf_coef)
    leaf_index = indices_of_leaves(leaf_place, leaf_pieces)
    near = near_rest(
        rest_index.reshape(-1),
        before,
        after,
        cells_of(before),
        cells_of(after),
        jnp.concatenate([table[0], table[2]], axis=0),
        own_cells,
        u,
    )
    down = parents_down(parent_index.reshape(-1), parent_pieces, parent_coupling, transfer)
    return finish(leaf_index.reshape(-1), leaf_pieces, leaf_coupling, down, basis, near)


def solution(mesh):
    in_specs = (
        P(None, ("leaf", "sib")),
        P(None, ("leaf", "sib")),
        P(("leaf", "sib"), None),
        P(("leaf", "sib"), None),
        P(("leaf", "sib"), None),
        P(("leaf", "sib"), None, None),
        P(("leaf", "sib"), None, None),
        P(("leaf", "sib"), None, None),
        P(("leaf", "sib"), None, None),
    )
    out_specs = P(None, ("leaf", "sib"))
    return jax.shard_map(body, mesh=mesh, in_specs=in_specs, out_specs=out_specs, check_vma=False)
```

```python
import functools
import math

import jax
import jax.numpy as jnp
import numpy as np
from jax import lax
from jax.experimental import pallas as pl
from jax.experimental.pallas import tpu as pltpu
from jax.sharding import PartitionSpec as P

CELLS = 256
NT = (((1,), (1,)), ((), ()))
NN = (((1,), (0,)), ((), ()))
VMEM_LIMIT = 56 * 1024 * 1024


def dot(a, b, dims):
    return lax.dot_general(a, b, dims, preferred_element_type=jnp.float32)


def kernel_table():
    cell = np.arange(CELLS)
    at_x, at_y = cell % 16, cell // 16
    blocks = []
    for step_y in range(-1, 2):
        for step_x in range(-1, 2):
            dx = (at_x[None, :] - at_x[:, None] - 16 * step_x).astype(np.float32)
            dy = (at_y[None, :] - at_y[:, None] - 16 * step_y).astype(np.float32)
            root = np.sqrt(dx * dx + dy * dy + np.float32(0.25))
            blocks.append(np.float32(4.0) / (np.float32(math.pi) * root))
    return np.stack(blocks).reshape(3, 3 * CELLS, CELLS).astype(jnp.bfloat16)


def low_lanes(rows):
    return lax.broadcasted_iota(jnp.int32, (rows, 128), 1) < 64


def one_hot(cells):
    hit = lax.broadcasted_iota(jnp.int32, (CELLS, cells.shape[1]), 0) == cells
    return jnp.where(hit, jnp.float32(1), jnp.float32(0)).astype(jnp.bfloat16)


def split(v):
    high = v.astype(jnp.bfloat16)
    low = (v - high.astype(jnp.float32)).astype(jnp.bfloat16)
    return high, low


def diagonal(y, sides):
    low = low_lanes(sides)
    left = jnp.where(low, y[:sides, :128], y[sides : 2 * sides, :128])
    right = jnp.where(low, y[2 * sides : 3 * sides, 128:], y[3 * sides :, 128:])
    return jnp.concatenate([left, right], axis=1)


def coef_kernel(x_ref, basis_ref, transfer_ref, leaf_ref, parent_ref):
    sides = x_ref.shape[0]
    low = low_lanes(sides)
    for pair in range(leaf_ref.shape[0] // 2):
        rows = []
        for p in (2 * pair, 2 * pair + 1):
            x4 = jnp.concatenate(
                [x_ref[:, (4 * p + c) * 128 : (4 * p + c + 1) * 128] for c in range(4)], axis=0
            )
            y = dot(x4, basis_ref[4 * p : 4 * p + 4].reshape(256, 128), NT)
            coef = diagonal(y, sides).astype(jnp.bfloat16)
            leaf_ref[p] = coef
            rows.append(coef)
        z = dot(
            jnp.concatenate(rows, axis=0),
            transfer_ref[2 * pair : 2 * pair + 2].reshape(128, 256),
            NT,
        )
        parent_ref[pair] = jnp.where(low, z[:sides], z[sides:]).astype(jnp.bfloat16)


def coefficients(x, basis, transfer):
    sides, parents = x.shape[0], transfer.shape[0]
    step = 8
    return pl.pallas_call(
        coef_kernel,
        grid=(parents // step,),
        in_specs=[
            pl.BlockSpec((sides, step * 512), lambda g: (0, g)),
            pl.BlockSpec((step * 4, 64, 128), lambda g: (g, 0, 0)),
            pl.BlockSpec((step, 64, 256), lambda g: (g, 0, 0)),
        ],
        out_specs=[
            pl.BlockSpec((step, sides, 256), lambda g: (g, 0, 0)),
            pl.BlockSpec((step // 2, sides, 128), lambda g: (g, 0, 0)),
        ],
        out_shape=[
            jax.ShapeDtypeStruct((parents, sides, 256), jnp.bfloat16),
            jax.ShapeDtypeStruct((parents // 2, sides, 128), jnp.bfloat16),
        ],
        compiler_params=pltpu.CompilerParams(vmem_limit_bytes=VMEM_LIMIT),
        cost_estimate=pl.CostEstimate(
            flops=1000000, bytes_accessed=1000, transcendentals=0
        ),
        name="coefficients",
    )(x, basis, transfer)


def scatter_row(charge_ref, base, x_ref, cells_ref):
    def group(first, carry):
        for extra in range(8):
            t = first * 8 + extra
            hot = one_hot(cells_ref[pl.ds(t, 1), :])
            y = dot(x_ref[:, pl.ds(pl.multiple_of(t * 128, 128), 128)], hot, NT)
            charge_ref[base + t] = y.astype(jnp.bfloat16)
        return carry

    lax.fori_loop(0, cells_ref.shape[0] // 8, group, 0)


def grid_field(index_ref, charge_ref, lhs_ref, table_ref, first, step):
    sides = charge_ref.shape[1]
    slots = table_ref.shape[0] // CELLS
    for t in range(step):
        for k in range(slots):
            lhs_ref[t * sides : (t + 1) * sides, k * CELLS : (k + 1) * CELLS] = charge_ref[
                index_ref[(first + t) * slots + k]
            ]
    return dot(lhs_ref[...], table_ref[...], NN).reshape(step, sides, CELLS)


def near_own_kernel(index_ref, x_ref, cells_ref, table_ref, u_ref, charge_ref, lhs_ref):
    leaves, step = cells_ref.shape[0], u_ref.shape[0]
    g = pl.program_id(0)

    @pl.when(g == 0)
    def _():
        charge_ref[leaves] = jnp.zeros(charge_ref.shape[1:], jnp.bfloat16)
        scatter_row(charge_ref, 0, x_ref, cells_ref)

    u_ref[...] = grid_field(index_ref, charge_ref, lhs_ref, table_ref, g * step, step)


def near_own(index, x, cells, table):
    sides, leaves = x.shape[0], cells.shape[0]
    step = 32
    return pl.pallas_call(
        near_own_kernel,
        grid=(leaves // step,),
        in_specs=[
            pl.BlockSpec(memory_space=pltpu.SMEM),
            pl.BlockSpec((sides, leaves * 128), lambda g: (0, 0)),
            pl.BlockSpec((leaves, 128), lambda g: (0, 0)),
            pl.BlockSpec(table.shape, lambda g: (0, 0)),
        ],
        out_specs=pl.BlockSpec((step, sides, CELLS), lambda g: (g, 0, 0)),
        out_shape=jax.ShapeDtypeStruct((leaves, sides, CELLS), jnp.float32),
        scratch_shapes=[
            pltpu.VMEM((leaves + 1, sides, CELLS), jnp.bfloat16),
            pltpu.VMEM((step * sides, table.shape[0]), jnp.bfloat16),
        ],
        compiler_params=pltpu.CompilerParams(vmem_limit_bytes=VMEM_LIMIT),
        cost_estimate=pl.CostEstimate(
            flops=1000000, bytes_accessed=1000, transcendentals=0
        ),
        name="near_own",
    )(index, x, cells, table)


def near_rest_kernel(
    index_ref, above_ref, below_ref, cells_above_ref, cells_below_ref, table_ref, cells_ref, u_ref, out_ref, charge_ref, lhs_ref
):
    leaves, step = cells_above_ref.shape[0], u_ref.shape[0]
    sides = u_ref.shape[1]
    g = pl.program_id(0)

    @pl.when(g == 0)
    def _():
        charge_ref[2 * leaves] = jnp.zeros(charge_ref.shape[1:], jnp.bfloat16)
        scatter_row(charge_ref, 0, above_ref, cells_above_ref)
        scatter_row(charge_ref, leaves, below_ref, cells_below_ref)

    u = u_ref[...] + grid_field(index_ref, charge_ref, lhs_ref, table_ref, g * step, step)
    for t in range(step):
        hot = one_hot(cells_ref[t : t + 1, :])
        near = dot(jnp.concatenate(split(u[t]), axis=0), hot, NN)
        out_ref[:, t * 128 : (t + 1) * 128] = near[:sides] + near[sides:]


def near_rest(index, above, below, cells_above, cells_below, table, cells, u):
    leaves, sides, _ = u.shape
    step = 32
    row = pl.BlockSpec((sides, leaves * 128), lambda g: (0, 0))
    row_cells = pl.BlockSpec((leaves, 128), lambda g: (0, 0))
    return pl.pallas_call(
        near_rest_kernel,
        grid=(leaves // step,),
        in_specs=[
            pl.BlockSpec(memory_space=pltpu.SMEM),
            row,
            row,
            row_cells,
            row_cells,
            pl.BlockSpec(table.shape, lambda g: (0, 0)),
            pl.BlockSpec((step, 128), lambda g: (g, 0)),
            pl.BlockSpec((step, sides, CELLS), lambda g: (g, 0, 0)),
        ],
        out_specs=pl.BlockSpec((sides, step * 128), lambda g: (0, g)),
        out_shape=jax.ShapeDtypeStruct((sides, leaves * 128), jnp.float32),
        scratch_shapes=[
            pltpu.VMEM((2 * leaves + 1, sides, CELLS), jnp.bfloat16),
            pltpu.VMEM((step * sides, table.shape[0]), jnp.bfloat16),
        ],
        compiler_params=pltpu.CompilerParams(vmem_limit_bytes=VMEM_LIMIT),
        cost_estimate=pl.CostEstimate(
            flops=25000000000, bytes_accessed=1000, transcendentals=0
        ),
        name="near_rest",
    )(index, above, below, cells_above, cells_below, table, cells, u)


def spread(table_ref, at, pair):
    low = low_lanes(pair.shape[0])
    wide = pair.astype(jnp.float32)
    turned = pltpu.roll(wide, 64, 1)
    table_ref[at] = jnp.where(low, wide, turned).astype(jnp.bfloat16)
    table_ref[at + 1] = jnp.where(low, turned, wide).astype(jnp.bfloat16)


def pick(table_ref, first, second):
    low = low_lanes(table_ref.shape[1])
    return jnp.where(low, table_ref[first], table_ref[second])


def parent_kernel(pieces, index_ref, *rest):
    pairs_refs = rest[:pieces]
    coupling_ref, transfer_ref, down_ref, table_ref, lhs_ref = rest[pieces:]
    count, sides, _ = down_ref.shape
    slots = coupling_ref.shape[2] // 64
    pairs = pairs_refs[0].shape[0]
    low = low_lanes(sides)
    g = pl.program_id(0)

    @pl.when(g == 0)
    def _():
        table_ref[2 * pieces * pairs] = jnp.zeros(table_ref.shape[1:], jnp.bfloat16)
        for number, pairs_ref in enumerate(pairs_refs):

            def group(first, carry):
                for extra in range(8):
                    at = first * 8 + extra
                    spread(table_ref, 2 * (number * pairs + at), pairs_ref[at])
                return carry

            lax.fori_loop(0, pairs // 8, group, 0)

    for pair in range(count // 2):
        for half in range(2):
            base = (g * count + 2 * pair + half) * slots
            rows = slice(half * sides, (half + 1) * sides)
            for j in range(slots // 2):
                lhs_ref[rows, j * 128 : (j + 1) * 128] = pick(
                    table_ref, index_ref[base + 2 * j], index_ref[base + 2 * j + 1]
                )
            if slots % 2:
                lhs_ref[rows, slots // 2 * 128 :] = table_ref[index_ref[base + slots - 1]]
        y = dot(
            lhs_ref[:, : slots * 64],
            coupling_ref[2 * pair : 2 * pair + 2].reshape(128, slots * 64),
            NT,
        )
        zero = jnp.zeros((sides, 128), jnp.float32)
        own = jnp.concatenate(
            [jnp.where(low, y[:sides], zero), jnp.where(low, zero, y[sides:])], axis=0
        ).astype(jnp.bfloat16)
        d = dot(own, transfer_ref[2 * pair : 2 * pair + 2].reshape(128, 256), NN)
        down_ref[2 * pair] = d[:sides]
        down_ref[2 * pair + 1] = d[sides:]


def parents_down(index, pieces, coupling, transfer):
    parents, _, width = coupling.shape
    pairs, sides, _ = pieces[0].shape
    step = 8
    return pl.pallas_call(
        functools.partial(parent_kernel, len(pieces)),
        grid=(parents // step,),
        in_specs=[
            pl.BlockSpec(memory_space=pltpu.SMEM),
        ]
        + [pl.BlockSpec(pieces[0].shape, lambda g: (0, 0, 0))] * len(pieces)
        + [
            pl.BlockSpec((step, 64, width), lambda g: (g, 0, 0)),
            pl.BlockSpec((step, 64, 256), lambda g: (g, 0, 0)),
        ],
        out_specs=pl.BlockSpec((step, sides, 256), lambda g: (g, 0, 0)),
        out_shape=jax.ShapeDtypeStruct((parents, sides, 256), jnp.float32),
        scratch_shapes=[
            pltpu.VMEM((2 * len(pieces) * pairs + 1, sides, 128), jnp.bfloat16),
            pltpu.VMEM((2 * sides, (width + 127) // 128 * 128), jnp.bfloat16),
        ],
        compiler_params=pltpu.CompilerParams(vmem_limit_bytes=VMEM_LIMIT),
        cost_estimate=pl.CostEstimate(
            flops=17000000000, bytes_accessed=1000, transcendentals=0
        ),
        name="parents_down",
    )(index, *pieces, coupling, transfer)


def final_kernel(pieces, index_ref, *rest):
    piece_refs = rest[:pieces]
    coupling_ref, down_ref, basis_ref, near_ref, out_ref, table_ref, lhs_ref = rest[pieces:]
    parents, sides, _ = down_ref.shape
    slots = coupling_ref.shape[2] // 64
    per_piece = piece_refs[0].shape[0]
    g = pl.program_id(0)

    @pl.when(g == 0)
    def _():
        table_ref[4 * pieces * per_piece] = jnp.zeros(table_ref.shape[1:], jnp.bfloat16)
        for number, piece_ref in enumerate(piece_refs):

            def group(first, carry):
                for extra in range(4):
                    p = first * 4 + extra
                    row = piece_ref[p]
                    at = (number * per_piece + p) * 4
                    spread(table_ref, at, row[:, :128])
                    spread(table_ref, at + 2, row[:, 128:])
                return carry

            lax.fori_loop(0, per_piece // 4, group, 0)

    low = low_lanes(sides)
    for p in range(parents):
        for c in range(4):
            base = (g * parents * 4 + 4 * p + c) * slots
            for j in range(slots // 2):
                lhs_ref[c * sides : (c + 1) * sides, j * 128 : (j + 1) * 128] = pick(
                    table_ref, index_ref[base + 2 * j], index_ref[base + 2 * j + 1]
                )
        y = dot(lhs_ref[...], coupling_ref[4 * p : 4 * p + 4].reshape(256, slots * 64), NT)
        total = diagonal(y, sides) + down_ref[p]
        left, right = total[:, :128], total[:, 128:]
        zero = jnp.zeros((sides, 128), jnp.float32)
        own = jnp.concatenate(
            [
                jnp.concatenate([jnp.where(low, left, zero), zero], axis=1),
                jnp.concatenate([jnp.where(low, zero, left), zero], axis=1),
                jnp.concatenate([zero, jnp.where(low, right, zero)], axis=1),
                jnp.concatenate([zero, jnp.where(low, zero, right)], axis=1),
            ],
            axis=0,
        ).astype(jnp.bfloat16)
        far = dot(own, basis_ref[4 * p : 4 * p + 4].reshape(256, 128), NN)
        for c in range(4):
            columns = slice((4 * p + c) * 128, (4 * p + c + 1) * 128)
            out_ref[:, columns] = far[c * sides : (c + 1) * sides] + near_ref[:, columns]


def finish(index, pieces, coupling, down, basis, near):
    leaves, _, width = coupling.shape
    sides = down.shape[1]
    step = 32
    whole = pl.BlockSpec(pieces[0].shape, lambda g: (0, 0, 0))
    return pl.pallas_call(
        functools.partial(final_kernel, len(pieces)),
        grid=(leaves // step,),
        in_specs=[pl.BlockSpec(memory_space=pltpu.SMEM)]
        + [whole] * len(pieces)
        + [
            pl.BlockSpec((step, 64, width), lambda g: (g, 0, 0)),
            pl.BlockSpec((step // 4, sides, 256), lambda g: (g, 0, 0)),
            pl.BlockSpec((step, 64, 128), lambda g: (g, 0, 0)),
            pl.BlockSpec((sides, step * 128), lambda g: (0, g)),
        ],
        out_specs=pl.BlockSpec((sides, step * 128), lambda g: (0, g)),
        out_shape=jax.ShapeDtypeStruct((sides, leaves * 128), jnp.float32),
        scratch_shapes=[
            pltpu.VMEM((len(pieces) * leaves + 1, sides, 128), jnp.bfloat16),
            pltpu.VMEM((4 * sides, width), jnp.bfloat16),
        ],
        compiler_params=pltpu.CompilerParams(vmem_limit_bytes=VMEM_LIMIT),
        cost_estimate=pl.CostEstimate(
            flops=18000000000, bytes_accessed=1000, transcendentals=0
        ),
        name="finish",
    )(index, *pieces, coupling, down, basis, near)


def gather_parents(pairs):
    sibs, at = lax.axis_size("sib"), lax.axis_index("sib")
    line = [pairs]
    for shift in range(1, sibs):
        turn = [(i, (i + shift) % sibs) for i in range(sibs)]
        line.append(lax.ppermute(pairs, "sib", turn))
    line = jnp.concatenate(line, axis=0)
    every = lax.all_gather(line, "leaf", axis=0, tiled=True)
    return [every], lambda leaf, sib: leaf * sibs + jnp.remainder(at - sib, sibs)


def gather_leaves(block):
    sibs, at = lax.axis_size("sib"), lax.axis_index("sib")
    turns = [
        lax.ppermute(block, "sib", [(i, (i + shift) % sibs) for i in range(sibs)])
        for shift in range(1, sibs)
    ]
    return [block] + turns, lambda sib: jnp.remainder(at - sib, sibs)


def body(
    points_x,
    coords,
    near_list,
    leaf_list,
    parent_list,
    basis,
    transfer,
    leaf_coupling,
    parent_coupling,
):
    sides = points_x.shape[0]
    leaves, rank_dim, leaf_size = basis.shape
    parents = leaves // 4
    everyone = ("leaf", "sib")
    devices = lax.axis_size("leaf") * lax.axis_size("sib")
    sibs = lax.axis_size("sib")
    table = jnp.asarray(kernel_table())

    packed_xy = coords.astype(jnp.bfloat16).reshape(sides, -1)
    packed = jnp.concatenate([points_x, packed_xy], axis=1)
    upward = [(i, i + 1) for i in range(devices - 1)]
    downward = [(j, i) for i, j in upward]
    before = lax.ppermute(packed, everyone, upward)
    after = lax.ppermute(packed, everyone, downward)

    leaf_coef, parent_pairs = coefficients(points_x, basis, transfer)
    parent_pieces, parent_place = gather_parents(parent_pairs)

    own_cells = (coords[1] * 16 + coords[0]).reshape(leaves, leaf_size)

    def cells_of(other):
        xy = other[:, leaves * leaf_size :].astype(jnp.int32).reshape(2, leaves, leaf_size)
        return xy[1] * 16 + xy[0]

    leaf_ids = jnp.arange(leaves, dtype=jnp.int32)[:, None]
    steps = jnp.arange(3, dtype=jnp.int32)[None, :] - 1
    own_list = near_list[:, 3:6]
    own_index = jnp.where(own_list >= 0, leaf_ids + steps, leaves)
    rest_list = jnp.concatenate([near_list[:, :3], near_list[:, 6:]], axis=1)
    rest_place = jnp.concatenate([leaf_ids + steps, leaves + leaf_ids + steps], axis=1)
    rest_index = jnp.where(rest_list >= 0, rest_place, 2 * leaves)

    owner = parent_list // parents
    parent_index = jnp.where(
        parent_list >= 0,
        parent_place(owner // sibs, owner % sibs) * parents + parent_list % parents,
        devices * parents,
    )

    def indices_of_leaves(leaf_place, leaf_pieces):
        local = leaf_list - lax.axis_index("leaf") * (sibs * leaves)
        return jnp.where(
            leaf_list >= 0,
            leaf_place(local // leaves) * leaves + local % leaves,
            len(leaf_pieces) * leaves,
        )

    u = near_own(own_index.reshape(-1), points_x, own_cells, table[1])
    leaf_coef, _ = lax.optimization_barrier((leaf_coef, (before, after)))
    leaf_pieces, leaf_place = gather_leaves(leaf_coef)
    leaf_index = indices_of_leaves(leaf_place, leaf_pieces)
    near = near_rest(
        rest_index.reshape(-1),
        before,
        after,
        cells_of(before),
        cells_of(after),
        jnp.concatenate([table[0], table[2]], axis=0),
        own_cells,
        u,
    )
    down = parents_down(parent_index.reshape(-1), parent_pieces, parent_coupling, transfer)
    return finish(leaf_index.reshape(-1), leaf_pieces, leaf_coupling, down, basis, near)


def solution(mesh):
    in_specs = (
        P(None, ("leaf", "sib")),
        P(None, ("leaf", "sib")),
        P(("leaf", "sib"), None),
        P(("leaf", "sib"), None),
        P(("leaf", "sib"), None),
        P(("leaf", "sib"), None, None),
        P(("leaf", "sib"), None, None),
        P(("leaf", "sib"), None, None),
        P(("leaf", "sib"), None, None),
    )
    out_specs = P(None, ("leaf", "sib"))
    return jax.shard_map(body, mesh=mesh, in_specs=in_specs, out_specs=out_specs, check_vma=False)
```

```python
import functools
import math

import jax
import jax.numpy as jnp
import numpy as np
from jax import lax
from jax.experimental import pallas as pl
from jax.experimental.pallas import tpu as pltpu
from jax.sharding import PartitionSpec as P

CELLS = 256
NT = (((1,), (1,)), ((), ()))
NN = (((1,), (0,)), ((), ()))
VMEM_LIMIT = 56 * 1024 * 1024


def dot(a, b, dims):
    return lax.dot_general(a, b, dims, preferred_element_type=jnp.float32)


def kernel_table():
    cell = np.arange(CELLS)
    at_x, at_y = cell % 16, cell // 16
    blocks = []
    for step_y in range(-1, 2):
        for step_x in range(-1, 2):
            dx = (at_x[None, :] - at_x[:, None] - 16 * step_x).astype(np.float32)
            dy = (at_y[None, :] - at_y[:, None] - 16 * step_y).astype(np.float32)
            root = np.sqrt(dx * dx + dy * dy + np.float32(0.25))
            blocks.append(np.float32(4.0) / (np.float32(math.pi) * root))
    return np.stack(blocks).reshape(3, 3 * CELLS, CELLS).astype(jnp.bfloat16)


def low_lanes(rows):
    return lax.broadcasted_iota(jnp.int32, (rows, 128), 1) < 64


def one_hot(cells):
    hit = lax.broadcasted_iota(jnp.int32, (CELLS, cells.shape[1]), 0) == cells
    return jnp.where(hit, jnp.float32(1), jnp.float32(0)).astype(jnp.bfloat16)


def split(v):
    high = v.astype(jnp.bfloat16)
    low = (v - high.astype(jnp.float32)).astype(jnp.bfloat16)
    return high, low


def diagonal(y, sides):
    low = low_lanes(sides)
    left = jnp.where(low, y[:sides, :128], y[sides : 2 * sides, :128])
    right = jnp.where(low, y[2 * sides : 3 * sides, 128:], y[3 * sides :, 128:])
    return jnp.concatenate([left, right], axis=1)


def coef_kernel(x_ref, basis_ref, transfer_ref, leaf_ref, parent_ref):
    sides = x_ref.shape[0]
    low = low_lanes(sides)
    for pair in range(leaf_ref.shape[0] // 2):
        rows = []
        for p in (2 * pair, 2 * pair + 1):
            x4 = jnp.concatenate(
                [x_ref[:, (4 * p + c) * 128 : (4 * p + c + 1) * 128] for c in range(4)], axis=0
            )
            y = dot(x4, basis_ref[4 * p : 4 * p + 4].reshape(256, 128), NT)
            coef = diagonal(y, sides).astype(jnp.bfloat16)
            leaf_ref[p] = coef
            rows.append(coef)
        z = dot(
            jnp.concatenate(rows, axis=0),
            transfer_ref[2 * pair : 2 * pair + 2].reshape(128, 256),
            NT,
        )
        parent_ref[pair] = jnp.where(low, z[:sides], z[sides:]).astype(jnp.bfloat16)


def coefficients(x, basis, transfer):
    sides, parents = x.shape[0], transfer.shape[0]
    step = 16
    return pl.pallas_call(
        coef_kernel,
        grid=(parents // step,),
        in_specs=[
            pl.BlockSpec((sides, step * 512), lambda g: (0, g)),
            pl.BlockSpec((step * 4, 64, 128), lambda g: (g, 0, 0)),
            pl.BlockSpec((step, 64, 256), lambda g: (g, 0, 0)),
        ],
        out_specs=[
            pl.BlockSpec((step, sides, 256), lambda g: (g, 0, 0)),
            pl.BlockSpec((step // 2, sides, 128), lambda g: (g, 0, 0)),
        ],
        out_shape=[
            jax.ShapeDtypeStruct((parents, sides, 256), jnp.bfloat16),
            jax.ShapeDtypeStruct((parents // 2, sides, 128), jnp.bfloat16),
        ],
        compiler_params=pltpu.CompilerParams(vmem_limit_bytes=VMEM_LIMIT),
        cost_estimate=pl.CostEstimate(
            flops=1000000, bytes_accessed=1000, transcendentals=0
        ),
        name="coefficients",
    )(x, basis, transfer)


def scatter_row(charge_ref, base, x_ref, cells_ref):
    sides = x_ref.shape[0]

    def group(first, carry):
        for extra in range(8):
            t = first * 8 + extra
            hot = one_hot(cells_ref[pl.ds(t, 1), :])
            y = dot(x_ref[:, pl.ds(pl.multiple_of(t * 128, 128), 128)], hot, NT)
            high, low = split(y)
            charge_ref[base + t, :sides] = high
            charge_ref[base + t, sides:] = low
        return carry

    lax.fori_loop(0, cells_ref.shape[0] // 8, group, 0)


def grid_field(index_ref, charge_ref, lhs_ref, table_ref, first, step):
    sides = charge_ref.shape[1] // 2
    slots = table_ref.shape[0] // CELLS
    for t in range(step):
        for k in range(slots):
            lhs_ref[t * 2 * sides : (t + 1) * 2 * sides, k * CELLS : (k + 1) * CELLS] = charge_ref[
                index_ref[(first + t) * slots + k]
            ]
    u = dot(lhs_ref[...], table_ref[...], NN).reshape(step, 2 * sides, CELLS)
    return u[:, :sides] + u[:, sides:]


def near_own_kernel(index_ref, x_ref, cells_ref, table_ref, u_ref, charge_ref, lhs_ref):
    leaves, step = cells_ref.shape[0], u_ref.shape[0]
    g = pl.program_id(0)

    @pl.when(g == 0)
    def _():
        charge_ref[leaves] = jnp.zeros(charge_ref.shape[1:], jnp.bfloat16)
        scatter_row(charge_ref, 0, x_ref, cells_ref)

    u_ref[...] = grid_field(index_ref, charge_ref, lhs_ref, table_ref, g * step, step)


def near_own(index, x, cells, table):
    sides, leaves = x.shape[0], cells.shape[0]
    step = 32
    return pl.pallas_call(
        near_own_kernel,
        grid=(leaves // step,),
        in_specs=[
            pl.BlockSpec(memory_space=pltpu.SMEM),
            pl.BlockSpec((sides, leaves * 128), lambda g: (0, 0)),
            pl.BlockSpec((leaves, 128), lambda g: (0, 0)),
            pl.BlockSpec(table.shape, lambda g: (0, 0)),
        ],
        out_specs=pl.BlockSpec((step, sides, CELLS), lambda g: (g, 0, 0)),
        out_shape=jax.ShapeDtypeStruct((leaves, sides, CELLS), jnp.float32),
        scratch_shapes=[
            pltpu.VMEM((leaves + 1, 2 * sides, CELLS), jnp.bfloat16),
            pltpu.VMEM((step * 2 * sides, table.shape[0]), jnp.bfloat16),
        ],
        compiler_params=pltpu.CompilerParams(vmem_limit_bytes=VMEM_LIMIT),
        cost_estimate=pl.CostEstimate(
            flops=1000000, bytes_accessed=1000, transcendentals=0
        ),
        name="near_own",
    )(index, x, cells, table)


def near_rest_kernel(
    index_ref, above_ref, below_ref, cells_above_ref, cells_below_ref, table_ref, cells_ref, u_ref, out_ref, charge_ref, lhs_ref
):
    leaves, step = cells_above_ref.shape[0], u_ref.shape[0]
    sides = u_ref.shape[1]
    g = pl.program_id(0)

    @pl.when(g == 0)
    def _():
        charge_ref[2 * leaves] = jnp.zeros(charge_ref.shape[1:], jnp.bfloat16)
        scatter_row(charge_ref, 0, above_ref, cells_above_ref)
        scatter_row(charge_ref, leaves, below_ref, cells_below_ref)

    u = u_ref[...] + grid_field(index_ref, charge_ref, lhs_ref, table_ref, g * step, step)
    for t in range(step):
        hot = one_hot(cells_ref[t : t + 1, :])
        near = dot(jnp.concatenate(split(u[t]), axis=0), hot, NN)
        out_ref[:, t * 128 : (t + 1) * 128] = near[:sides] + near[sides:]


def near_rest(index, above, below, cells_above, cells_below, table, cells, u):
    leaves, sides, _ = u.shape
    step = 32
    row = pl.BlockSpec((sides, leaves * 128), lambda g: (0, 0))
    row_cells = pl.BlockSpec((leaves, 128), lambda g: (0, 0))
    return pl.pallas_call(
        near_rest_kernel,
        grid=(leaves // step,),
        in_specs=[
            pl.BlockSpec(memory_space=pltpu.SMEM),
            row,
            row,
            row_cells,
            row_cells,
            pl.BlockSpec(table.shape, lambda g: (0, 0)),
            pl.BlockSpec((step, 128), lambda g: (g, 0)),
            pl.BlockSpec((step, sides, CELLS), lambda g: (g, 0, 0)),
        ],
        out_specs=pl.BlockSpec((sides, step * 128), lambda g: (0, g)),
        out_shape=jax.ShapeDtypeStruct((sides, leaves * 128), jnp.float32),
        scratch_shapes=[
            pltpu.VMEM((2 * leaves + 1, 2 * sides, CELLS), jnp.bfloat16),
            pltpu.VMEM((step * 2 * sides, table.shape[0]), jnp.bfloat16),
        ],
        compiler_params=pltpu.CompilerParams(vmem_limit_bytes=VMEM_LIMIT),
        cost_estimate=pl.CostEstimate(
            flops=25000000000, bytes_accessed=1000, transcendentals=0
        ),
        name="near_rest",
    )(index, above, below, cells_above, cells_below, table, cells, u)


def spread(table_ref, at, pair):
    low = low_lanes(pair.shape[0])
    wide = pair.astype(jnp.float32)
    turned = pltpu.roll(wide, 64, 1)
    table_ref[at] = jnp.where(low, wide, turned).astype(jnp.bfloat16)
    table_ref[at + 1] = jnp.where(low, turned, wide).astype(jnp.bfloat16)


def pick(table_ref, first, second):
    low = low_lanes(table_ref.shape[1])
    return jnp.where(low, table_ref[first], table_ref[second])


def parent_kernel(pieces, index_ref, *rest):
    pairs_refs = rest[:pieces]
    coupling_ref, transfer_ref, down_ref, table_ref, lhs_ref = rest[pieces:]
    count, sides, _ = down_ref.shape
    slots = coupling_ref.shape[2] // 64
    pairs = pairs_refs[0].shape[0]
    low = low_lanes(sides)
    g = pl.program_id(0)

    @pl.when(g == 0)
    def _():
        table_ref[2 * pieces * pairs] = jnp.zeros(table_ref.shape[1:], jnp.bfloat16)
        for number, pairs_ref in enumerate(pairs_refs):

            def group(first, carry):
                for extra in range(8):
                    at = first * 8 + extra
                    spread(table_ref, 2 * (number * pairs + at), pairs_ref[at])
                return carry

            lax.fori_loop(0, pairs // 8, group, 0)

    for pair in range(count // 2):
        for half in range(2):
            base = (g * count + 2 * pair + half) * slots
            rows = slice(half * sides, (half + 1) * sides)
            for j in range(slots // 2):
                lhs_ref[rows, j * 128 : (j + 1) * 128] = pick(
                    table_ref, index_ref[base + 2 * j], index_ref[base + 2 * j + 1]
                )
            if slots % 2:
                lhs_ref[rows, slots // 2 * 128 :] = table_ref[index_ref[base + slots - 1]]
        y = dot(
            lhs_ref[:, : slots * 64],
            coupling_ref[2 * pair : 2 * pair + 2].reshape(128, slots * 64),
            NT,
        )
        zero = jnp.zeros((sides, 128), jnp.float32)
        own = jnp.concatenate(
            [jnp.where(low, y[:sides], zero), jnp.where(low, zero, y[sides:])], axis=0
        ).astype(jnp.bfloat16)
        d = dot(own, transfer_ref[2 * pair : 2 * pair + 2].reshape(128, 256), NN)
        down_ref[2 * pair] = d[:sides]
        down_ref[2 * pair + 1] = d[sides:]


def parents_down(index, pieces, coupling, transfer):
    parents, _, width = coupling.shape
    pairs, sides, _ = pieces[0].shape
    step = 8
    return pl.pallas_call(
        functools.partial(parent_kernel, len(pieces)),
        grid=(parents // step,),
        in_specs=[
            pl.BlockSpec(memory_space=pltpu.SMEM),
        ]
        + [pl.BlockSpec(pieces[0].shape, lambda g: (0, 0, 0))] * len(pieces)
        + [
            pl.BlockSpec((step, 64, width), lambda g: (g, 0, 0)),
            pl.BlockSpec((step, 64, 256), lambda g: (g, 0, 0)),
        ],
        out_specs=pl.BlockSpec((step, sides, 256), lambda g: (g, 0, 0)),
        out_shape=jax.ShapeDtypeStruct((parents, sides, 256), jnp.float32),
        scratch_shapes=[
            pltpu.VMEM((2 * len(pieces) * pairs + 1, sides, 128), jnp.bfloat16),
            pltpu.VMEM((2 * sides, (width + 127) // 128 * 128), jnp.bfloat16),
        ],
        compiler_params=pltpu.CompilerParams(vmem_limit_bytes=VMEM_LIMIT),
        cost_estimate=pl.CostEstimate(
            flops=17000000000, bytes_accessed=1000, transcendentals=0
        ),
        name="parents_down",
    )(index, *pieces, coupling, transfer)


def final_kernel(pieces, index_ref, *rest):
    piece_refs = rest[:pieces]
    coupling_ref, down_ref, basis_ref, near_ref, out_ref, table_ref, lhs_ref = rest[pieces:]
    parents, sides, _ = down_ref.shape
    slots = coupling_ref.shape[2] // 64
    per_piece = piece_refs[0].shape[0]
    g = pl.program_id(0)

    @pl.when(g == 0)
    def _():
        table_ref[4 * pieces * per_piece] = jnp.zeros(table_ref.shape[1:], jnp.bfloat16)
        for number, piece_ref in enumerate(piece_refs):

            def group(first, carry):
                for extra in range(4):
                    p = first * 4 + extra
                    row = piece_ref[p]
                    at = (number * per_piece + p) * 4
                    spread(table_ref, at, row[:, :128])
                    spread(table_ref, at + 2, row[:, 128:])
                return carry

            lax.fori_loop(0, per_piece // 4, group, 0)

    low = low_lanes(sides)
    for p in range(parents):
        for c in range(4):
            base = (g * parents * 4 + 4 * p + c) * slots
            for j in range(slots // 2):
                lhs_ref[c * sides : (c + 1) * sides, j * 128 : (j + 1) * 128] = pick(
                    table_ref, index_ref[base + 2 * j], index_ref[base + 2 * j + 1]
                )
        y = dot(lhs_ref[...], coupling_ref[4 * p : 4 * p + 4].reshape(256, slots * 64), NT)
        total = diagonal(y, sides) + down_ref[p]
        left, right = total[:, :128], total[:, 128:]
        zero = jnp.zeros((sides, 128), jnp.float32)
        own = jnp.concatenate(
            [
                jnp.concatenate([jnp.where(low, left, zero), zero], axis=1),
                jnp.concatenate([jnp.where(low, zero, left), zero], axis=1),
                jnp.concatenate([zero, jnp.where(low, right, zero)], axis=1),
                jnp.concatenate([zero, jnp.where(low, zero, right)], axis=1),
            ],
            axis=0,
        ).astype(jnp.bfloat16)
        far = dot(own, basis_ref[4 * p : 4 * p + 4].reshape(256, 128), NN)
        for c in range(4):
            columns = slice((4 * p + c) * 128, (4 * p + c + 1) * 128)
            out_ref[:, columns] = far[c * sides : (c + 1) * sides] + near_ref[:, columns]


def finish(index, pieces, coupling, down, basis, near):
    leaves, _, width = coupling.shape
    sides = down.shape[1]
    step = 32
    whole = pl.BlockSpec(pieces[0].shape, lambda g: (0, 0, 0))
    return pl.pallas_call(
        functools.partial(final_kernel, len(pieces)),
        grid=(leaves // step,),
        in_specs=[pl.BlockSpec(memory_space=pltpu.SMEM)]
        + [whole] * len(pieces)
        + [
            pl.BlockSpec((step, 64, width), lambda g: (g, 0, 0)),
            pl.BlockSpec((step // 4, sides, 256), lambda g: (g, 0, 0)),
            pl.BlockSpec((step, 64, 128), lambda g: (g, 0, 0)),
            pl.BlockSpec((sides, step * 128), lambda g: (0, g)),
        ],
        out_specs=pl.BlockSpec((sides, step * 128), lambda g: (0, g)),
        out_shape=jax.ShapeDtypeStruct((sides, leaves * 128), jnp.float32),
        scratch_shapes=[
            pltpu.VMEM((len(pieces) * leaves + 1, sides, 128), jnp.bfloat16),
            pltpu.VMEM((4 * sides, width), jnp.bfloat16),
        ],
        compiler_params=pltpu.CompilerParams(vmem_limit_bytes=VMEM_LIMIT),
        cost_estimate=pl.CostEstimate(
            flops=18000000000, bytes_accessed=1000, transcendentals=0
        ),
        name="finish",
    )(index, *pieces, coupling, down, basis, near)


def gather_parents(pairs):
    sibs, at = lax.axis_size("sib"), lax.axis_index("sib")
    line = [pairs]
    for shift in range(1, sibs):
        turn = [(i, (i + shift) % sibs) for i in range(sibs)]
        line.append(lax.ppermute(pairs, "sib", turn))
    line = jnp.concatenate(line, axis=0)
    every = lax.all_gather(line, "leaf", axis=0, tiled=True)
    return [every], lambda leaf, sib: leaf * sibs + jnp.remainder(at - sib, sibs)


def gather_leaves(block):
    sibs, at = lax.axis_size("sib"), lax.axis_index("sib")
    turns = [
        lax.ppermute(block, "sib", [(i, (i + shift) % sibs) for i in range(sibs)])
        for shift in range(1, sibs)
    ]
    return [block] + turns, lambda sib: jnp.remainder(at - sib, sibs)


def body(
    points_x,
    coords,
    near_list,
    leaf_list,
    parent_list,
    basis,
    transfer,
    leaf_coupling,
    parent_coupling,
):
    sides = points_x.shape[0]
    leaves, rank_dim, leaf_size = basis.shape
    parents = leaves // 4
    everyone = ("leaf", "sib")
    devices = lax.axis_size("leaf") * lax.axis_size("sib")
    sibs = lax.axis_size("sib")
    table = jnp.asarray(kernel_table())

    packed_xy = coords.astype(jnp.bfloat16).reshape(sides, -1)
    packed = jnp.concatenate([points_x, packed_xy], axis=1)
    upward = [(i, i + 1) for i in range(devices - 1)]
    downward = [(j, i) for i, j in upward]
    before = lax.ppermute(packed, everyone, upward)
    after = lax.ppermute(packed, everyone, downward)

    leaf_coef, parent_pairs = coefficients(points_x, basis, transfer)
    parent_pieces, parent_place = gather_parents(parent_pairs)

    own_cells = (coords[1] * 16 + coords[0]).reshape(leaves, leaf_size)

    def cells_of(other):
        xy = other[:, leaves * leaf_size :].astype(jnp.int32).reshape(2, leaves, leaf_size)
        return xy[1] * 16 + xy[0]

    leaf_ids = jnp.arange(leaves, dtype=jnp.int32)[:, None]
    steps = jnp.arange(3, dtype=jnp.int32)[None, :] - 1
    own_list = near_list[:, 3:6]
    own_index = jnp.where(own_list >= 0, leaf_ids + steps, leaves)
    rest_list = jnp.concatenate([near_list[:, :3], near_list[:, 6:]], axis=1)
    rest_place = jnp.concatenate([leaf_ids + steps, leaves + leaf_ids + steps], axis=1)
    rest_index = jnp.where(rest_list >= 0, rest_place, 2 * leaves)

    owner = parent_list // parents
    parent_index = jnp.where(
        parent_list >= 0,
        parent_place(owner // sibs, owner % sibs) * parents + parent_list % parents,
        devices * parents,
    )

    def indices_of_leaves(leaf_place, leaf_pieces):
        local = leaf_list - lax.axis_index("leaf") * (sibs * leaves)
        return jnp.where(
            leaf_list >= 0,
            leaf_place(local // leaves) * leaves + local % leaves,
            len(leaf_pieces) * leaves,
        )

    u = near_own(own_index.reshape(-1), points_x, own_cells, table[1])
    leaf_coef, _ = lax.optimization_barrier((leaf_coef, (before, after)))
    leaf_pieces, leaf_place = gather_leaves(leaf_coef)
    leaf_index = indices_of_leaves(leaf_place, leaf_pieces)
    near = near_rest(
        rest_index.reshape(-1),
        before,
        after,
        cells_of(before),
        cells_of(after),
        jnp.concatenate([table[0], table[2]], axis=0),
        own_cells,
        u,
    )
    down = parents_down(parent_index.reshape(-1), parent_pieces, parent_coupling, transfer)
    return finish(leaf_index.reshape(-1), leaf_pieces, leaf_coupling, down, basis, near)


def solution(mesh):
    in_specs = (
        P(None, ("leaf", "sib")),
        P(None, ("leaf", "sib")),
        P(("leaf", "sib"), None),
        P(("leaf", "sib"), None),
        P(("leaf", "sib"), None),
        P(("leaf", "sib"), None, None),
        P(("leaf", "sib"), None, None),
        P(("leaf", "sib"), None, None),
        P(("leaf", "sib"), None, None),
    )
    out_specs = P(None, ("leaf", "sib"))
    return jax.shard_map(body, mesh=mesh, in_specs=in_specs, out_specs=out_specs, check_vma=False)
```
